32 devices in a mesh: tm: 8 (over z, y), height: 4 (over x, core).
Axes of the slice: x: 2, y: 2, z: 4, core: 2. Of those that a mesh axis runs over, the one named last changes fastest.
Arguments:
- latents: bfloat16 [16, 16, 128, 256], P('tm', 'height'), may hold values from -6 to 6
- conv_first: bfloat16 [3, 3, 3, 256, 256], replicated, may hold values from -0.078125 to 0.078125
- conv_second: bfloat16 [3, 3, 3, 256, 256], replicated, may hold values from -0.078125 to 0.078125
- codebook: bfloat16 [262144, 256], P('height'), may hold values from -13 to 13
- codes: int32 [16, 16, 128], P('tm', 'height'), may hold values from 0 to 262143, as said below
- upstream: bfloat16 [16, 16, 128, 256], P('tm', 'height'), may hold values from -6 to 6
Outputs:
- grad_latent: bfloat16 [16, 16, 128, 256], P('tm', 'height')
- codebook_grad: bfloat16 [262144, 256], P(('height', 'tm'))
The draws below stay inside these ranges and needn't reach their ends.
Inputs may be any that keep to these rules, and one draw needn't show every extreme that they name: Each device's 1024 cells hold at most 64 codes of any one aligned range of 8192 codes; some ranges receive exactly 64 from every device.
All inputs are finite; a program needn't handle non-finite values.
Results may differ from the reference program's by a relative error of at most 0.0085.
Values may be sent and summed in bfloat16 or wider, within the bound.
No kernel may reach another device: no remote copies, remote signals or barrier semaphores. Data moves between devices by JAX's collectives and lax.ppermute only.
A program may use at most 128 MiB of HBM per device.

```python
import jax
import jax.numpy as jnp
from jax import lax

C = 256
K = 262144
T_DEV = 2
H_DEV = 4
W = 128
TT = 16
HH = 16
CELLS_DEV = 1024
CAP = 64
K_OWN = 8192
N_TM = 8
N_HEIGHT = 4


def draw_codebook(key, part):
    key_base, key_col, key_row = jax.random.split(key, 3)
    column_scale = jnp.exp(jax.random.uniform(key_col, (1, C), jnp.float32, -1.15, 1.15))
    row_scale = jnp.exp(jax.random.uniform(key_row, (K, 1), jnp.float32, -0.7, 0.7))
    base = jnp.clip(jax.random.normal(key_base, (K, C), jnp.float32), -4.0, 4.0)
    values = base * row_scale * column_scale * 0.5
    return values.astype(jnp.bfloat16)


def draw_codes(key, part):
    owners = N_TM * N_HEIGHT
    slots = owners * CAP
    key_rank, key_noise, key_order, key_first, key_second = jax.random.split(key, 5)
    ranking = jax.random.permutation(key_rank, owners).astype(jnp.int32)
    priority = jnp.where(ranking < owners // 8, 4096, ranking * 256 // owners).astype(jnp.int32)
    slot_owner = (jnp.arange(slots, dtype=jnp.int32) // CAP).astype(jnp.int32)
    noise = jax.random.randint(key_noise, (owners, slots), 0, 1024, dtype=jnp.int32)
    score = (priority[slot_owner][None, :] + noise) * slots + jnp.arange(slots, dtype=jnp.int32)[None, :]
    picked = lax.top_k(score, CELLS_DEV)[1].astype(jnp.int32)
    chosen = slot_owner[picked]
    order_keys = jax.random.split(key_order, owners)
    order = jax.vmap(lambda order_key: jax.random.permutation(order_key, CELLS_DEV).astype(jnp.int32))(order_keys)
    chosen = jnp.take_along_axis(chosen, order, 1)
    offset = jnp.minimum(jax.random.randint(key_first, (owners, CELLS_DEV), 0, K_OWN, dtype=jnp.int32), jax.random.randint(key_second, (owners, CELLS_DEV), 0, K_OWN, dtype=jnp.int32))
    values = chosen * K_OWN + offset
    values = values.reshape(N_TM, N_HEIGHT, T_DEV, H_DEV, W).transpose(0, 2, 1, 3, 4)
    return values.reshape(TT, HH, W).astype(jnp.int32)


def block_levels(key, extent, cuts, low, largest):
    def one(axis_at, parts):
        steps = jax.random.uniform(jax.random.fold_in(jax.random.fold_in(key, 6), axis_at), (parts,), jnp.float32, low / len(cuts), largest / len(cuts))
        return jnp.repeat(jnp.exp(steps), extent[axis_at] // parts).reshape((-1,) + (1,) * (len(extent) - axis_at - 1))

    factor_of = one(*cuts[0])
    for cut in cuts[1:]:
        factor_of = factor_of * one(*cut)
    return factor_of


def gaussian(own_key, dims, scale, bound, cuts=(), kind=jnp.bfloat16):
    level = block_levels(own_key, dims, cuts, -0.22, 0.18) if cuts else 1.0
    array = jax.random.normal(own_key, dims, jnp.float32) * scale * level
    return jnp.minimum(jnp.maximum(array, -bound), bound).astype(kind)


def setup_inputs(seed: int = 0) -> dict:
    arg_keys = jax.random.split(jax.random.key(seed), 7)
    latents = gaussian(arg_keys[0], (TT, HH, W, C), 1.0, 6.0, ((0, 8), (1, 4)))
    conv_first = gaussian(arg_keys[1], (3, 3, 3, C, C), (27 * C) ** -0.5, 0.078125)
    conv_second = gaussian(arg_keys[2], (3, 3, 3, C, C), (27 * C) ** -0.5, 0.078125)
    codebook = draw_codebook(jax.random.fold_in(arg_keys[6], 71), 0)
    codes = draw_codes(jax.random.fold_in(arg_keys[6], 71), 0)
    upstream = gaussian(arg_keys[5], (TT, HH, W, C), 1.0, 6.0, ((0, 8), (1, 4)))
    return {"latents": latents, "conv_first": conv_first, "conv_second": conv_second, "codebook": codebook, "codes": codes, "upstream": upstream}


COMMIT = 0.25

def norm_act(video):
    values = video.astype(jnp.float32)
    scaled = values * lax.rsqrt(lax.optimization_barrier(jnp.mean(values * values, -1, keepdims=True)) + 1e-06)
    return jax.nn.silu(scaled).astype(jnp.bfloat16)

def conv_block(video, weight):
    active = norm_act(video)
    padded = jnp.pad(active, ((2, 0), (1, 1), (1, 1), (0, 0)))
    flat_weight = weight.reshape(27 * C, C)

    def one_frame(frame):
        window = lax.dynamic_slice_in_dim(padded, frame.astype(jnp.int32), 3, 0)
        pieces = [window[step_t, step_h:step_h + HH, step_w:step_w + W, :] for step_t in range(3) for step_h in range(3) for step_w in range(3)]
        patch = jnp.concatenate(pieces, -1).reshape(HH * W, 27 * C)
        return jnp.dot(patch, flat_weight, preferred_element_type=jnp.float32).reshape(HH, W, C)
    conv = lax.map(one_frame, jnp.arange(TT, dtype=jnp.int32))
    return (video.astype(jnp.float32) + conv).astype(jnp.bfloat16)

def rotate_back(latent, quant, upward):
    lat_norm = jnp.sqrt(lax.optimization_barrier(jnp.sum(latent * latent, -1, keepdims=True)) + 1e-06)
    quant_norm = jnp.sqrt(lax.optimization_barrier(jnp.sum(quant * quant, -1, keepdims=True)) + 1e-06)
    lat_unit = latent / lat_norm
    quant_unit = quant / quant_norm
    cosine = lax.optimization_barrier(jnp.sum(lat_unit * quant_unit, -1, keepdims=True))
    summed = lat_unit + quant_unit
    turned = upward - summed * (lax.optimization_barrier(jnp.sum(summed * upward, -1, keepdims=True)) / (1.0 + cosine))
    turned = turned + 2.0 * lat_unit * lax.optimization_barrier(jnp.sum(quant_unit * upward, -1, keepdims=True))
    return quant_norm / lat_norm * turned + 2.0 * COMMIT * (latent - quant)

def reference(latents, conv_first, conv_second, codebook, codes, upstream):
    first = conv_block(latents, conv_first)
    encoded = conv_block(first, conv_second)
    code_flat = codes.reshape(-1).astype(jnp.int32)
    latent_flat = encoded.reshape(-1, C).astype(jnp.float32)
    quant = jnp.take(codebook, code_flat, axis=0).astype(jnp.float32)
    upward = upstream.reshape(-1, C).astype(jnp.float32)
    grad_flat = rotate_back(latent_flat, quant, upward)
    diff = lax.optimization_barrier((quant - latent_flat).astype(jnp.bfloat16))
    sums = jax.ops.segment_sum(diff.astype(jnp.float32), code_flat, num_segments=K)
    grad_latent = grad_flat.astype(jnp.bfloat16).reshape(upstream.shape)
    return (grad_latent, (2.0 * sums).astype(jnp.bfloat16))
```

```python
import functools

import jax
import jax.numpy as jnp
from jax import lax
from jax.experimental import pallas as pl
from jax.experimental.pallas import tpu as pltpu
from jax.sharding import PartitionSpec as P

COMMIT = 0.25
BATCH = 64
TILE = 16
F32 = jnp.float32
BF16 = jnp.bfloat16
VMEM = pl.BlockSpec(memory_space=pltpu.VMEM)
SMEM = pl.BlockSpec(memory_space=pltpu.SMEM)
HBM = pl.BlockSpec(memory_space=pl.ANY)
NT = (((1,), (1,)), ((), ()))


def along(x, axis, by):
    count = lax.axis_size(axis)
    return lax.ppermute(x, axis, [(i, i + by) for i in range(count) if 0 <= i + by < count])


def around(x, axis, by):
    count = lax.axis_size(axis)
    return lax.ppermute(x, axis, [(i, (i + by) % count) for i in range(count)])


def params(megabytes):
    return pltpu.CompilerParams(vmem_limit_bytes=megabytes << 20)


def act(values):
    scaled = values * lax.rsqrt(jnp.mean(values * values, -1, keepdims=True) + 1e-06)
    return scaled / (1.0 + jnp.exp(-scaled))


def lanes(block):
    return jnp.concatenate([block[i : i + 1, :] for i in range(block.shape[0])], axis=1)


def onehot(mask):
    return jnp.where(mask, 1.0, 0.0).astype(BF16)


def index_kernel(groups, tiles, held, capacity, where_ref, codes_ref, ask_ref, low_ref, send_ref, place_ref):
    lines, width = codes_ref.shape[1:]
    cells = lines * width
    owners = groups * tiles
    range_rows = held // tiles
    block_slots = tiles * capacity
    batches = block_slots // BATCH
    here = where_ref[0]
    own = lanes(codes_ref[here])
    block = own // range_rows
    target = block % tiles * groups + block // tiles
    home = own // held
    arrival = lax.rem(here - home + groups, groups)
    peers = [lanes(codes_ref[lax.rem(here + k, groups)]) for k in range(groups)]
    own_hits = lax.broadcasted_iota(jnp.int32, (owners, cells), 0) == target
    home_hits = lax.broadcasted_iota(jnp.int32, (groups, cells), 0) == arrival
    peer_hits = [peer // held == here for peer in peers]
    hits = jnp.concatenate(
        [jnp.where(own_hits, 1.0, 0.0), jnp.where(home_hits, 1.0, 0.0)] + [jnp.where(x, 1.0, 0.0) for x in peer_hits], axis=0
    )
    count = hits.shape[0]
    pad = -count % 16
    if pad:
        hits = jnp.concatenate([hits, jnp.zeros((pad, cells), F32)], axis=0)
    earlier = onehot(
        lax.broadcasted_iota(jnp.int32, (width, width), 0) < lax.broadcasted_iota(jnp.int32, (width, width), 1)
    )
    before = jnp.zeros((count + pad, 1), F32)
    parts = []
    for i in range(lines):
        part = hits[:, i * width : (i + 1) * width]
        parts.append(jnp.dot(part.astype(BF16), earlier, preferred_element_type=F32) + before)
        before = before + jnp.sum(part, 1, keepdims=True)
    ranks = jnp.concatenate(parts, axis=1)
    own_rank = jnp.sum(ranks[:owners] * hits[:owners], 0, keepdims=True)
    home_rank = jnp.sum(ranks[owners : owners + groups] * hits[owners : owners + groups], 0, keepdims=True)
    place_ref[0:1, :] = target.astype(F32) * capacity + own_rank
    place_ref[1:2, :] = arrival.astype(F32) * block_slots + home_rank
    place_ref[2:, :] = jnp.zeros((6, cells), F32)
    local = own % range_rows
    own_ones = hits[:owners]
    picked = jnp.concatenate(
        [own_ones * (local // 256).astype(F32), own_ones * (local % 256).astype(F32), own_ones], axis=0
    ).astype(BF16)
    chosen = onehot(lax.broadcasted_iota(jnp.int32, (capacity, cells), 0).astype(F32) == own_rank)
    slots = lax.dot_general(picked, chosen, NT, preferred_element_type=F32)
    code = slots[:owners] * 256.0 + slots[owners : 2 * owners]
    send_ref[...] = jnp.where(slots[2 * owners :] > 0.5, code, -1.0).astype(jnp.int32)
    columns = []
    for k in range(groups):
        hit = hits[owners + groups + k : owners + groups + k + 1]
        rank = ranks[owners + groups + k : owners + groups + k + 1].astype(jnp.int32)
        row = jnp.where(peer_hits[k], peers[k] - here * held, 0)
        batch = onehot(
            lax.broadcasted_iota(jnp.int32, (batches, cells), 0) == jnp.where(peer_hits[k], rank // BATCH, -1)
        ).astype(F32)
        tile = row // TILE
        picked = jnp.concatenate(
            [
                batch * (tile // 128).astype(F32),
                batch * (tile % 128).astype(F32),
                batch,
                batch * (row % TILE).astype(F32),
            ],
            axis=0,
        ).astype(BF16)
        chosen = onehot(lax.broadcasted_iota(jnp.int32, (BATCH, cells), 0) == rank % BATCH)
        slots = lax.dot_general(picked, chosen, NT, preferred_element_type=F32)
        asked = slots[:batches] * 128.0 + slots[batches : 2 * batches]
        ask_ref[k * batches : (k + 1) * batches, :] = jnp.where(
            slots[2 * batches : 3 * batches] > 0.5, asked, -1.0
        ).astype(jnp.int32)
        columns.append(lax.dot_general(chosen, picked[3 * batches :], NT, preferred_element_type=F32))
    low_ref[...] = jnp.concatenate(columns, axis=1)


def gather_kernel(batches, ask_ref, book_ref, low_ref, *refs):
    outs, land, sems = refs[:-2], refs[-2], refs[-1]
    total = len(outs) * batches

    def copy_in(g):
        def one(i, carry):
            tile = jnp.maximum(ask_ref[g, i], 0)
            pltpu.make_async_copy(book_ref.at[tile], land.at[g * BATCH + i], sems.at[g]).start()
            return carry

        lax.fori_loop(0, BATCH, one, 0, unroll=16)

    for g in range(total):
        pl.when(ask_ref[g, 0] >= 0)(functools.partial(copy_in, g))
    at = lax.broadcasted_iota(jnp.int32, (BATCH, BATCH * TILE), 1)
    at = at - TILE * lax.broadcasted_iota(jnp.int32, (BATCH, BATCH * TILE), 0)
    at = at.astype(F32)
    for g in range(total):
        out = outs[g // batches]
        span = slice(g % batches * BATCH, (g % batches + 1) * BATCH)
        filled = ask_ref[g, 0] >= 0

        @pl.when(filled)
        def _(g=g, out=out, span=span):
            block = land.at[pl.ds(g * BATCH, BATCH)]
            pltpu.make_async_copy(book_ref.at[pl.ds(0, BATCH)], block, sems.at[g]).wait()
            tiles = land[g * BATCH : (g + 1) * BATCH].reshape(BATCH * TILE, land.shape[-1])
            out[span, :] = jnp.dot(onehot(at == low_ref[:, g : g + 1]), tiles, preferred_element_type=F32).astype(BF16)

        @pl.when(jnp.logical_not(filled))
        def _(out=out, span=span):
            out[span, :] = jnp.zeros((BATCH, out.shape[-1]), BF16)


def convolve(window, weight_ref, frame):
    rows, columns, channels = window.shape[1] - 2, window.shape[2], window.shape[3]
    flat = rows * columns
    pieces = [window[frame + p, q : q + rows].reshape(flat, channels) for p in range(3) for q in range(3)]
    patch = jnp.concatenate(pieces, axis=1)
    place = lax.broadcasted_iota(jnp.int32, (flat, 1), 0) % columns
    sums = [
        jnp.dot(patch, weight_ref[:, :, r].reshape(9 * channels, channels), preferred_element_type=F32)
        for r in range(3)
    ]
    left = jnp.where(place == 0, 0.0, pltpu.roll(sums[0], 1, 0))
    right = jnp.where(place == columns - 1, 0.0, pltpu.roll(sums[2], flat - 1, 0))
    return sums[1] + left + right


def fill_window(window, own, before, sides, corners, change):
    window[0:2, 1:2] = change(before[0][...])
    window[0:2, 2:-2] = change(before[1][...])
    window[0:2, -2:-1] = change(before[2][...])
    window[0:2, 0:1] = change(corners[0][...])
    window[0:2, -1:] = change(corners[1][...])
    window[2:4, 0:1] = change(sides[0][...])
    window[2:4, -1:] = change(sides[1][...])
    if len(own) == 1:
        window[2:4, 1:-1] = change(own[0][...])
    else:
        window[2:4, 1:2] = change(own[0][...])
        window[2:4, 2:-2] = change(own[1][...])
        window[2:4, -2:-1] = change(own[2][...])


def first_kernel(video, b0, b1, b2, s0, s1, c0, c1, weight, first, top, mid, bottom, window):
    fill_window(window, (video,), (b0, b1, b2), (s0, s1), (c0, c1), lambda x: act(x.astype(F32)).astype(BF16))
    frames, rows, columns, channels = video.shape
    for f in range(frames):
        conv = convolve(window, weight, f).reshape(rows, columns, channels)
        result = (video[f].astype(F32) + conv).astype(BF16)
        first[f] = result
        active = act(result.astype(F32)).astype(BF16)
        top[f] = active[0:1]
        mid[f] = active[1:-1]
        bottom[f] = active[-1:]


def second_kernel(
    first, o0, o1, o2, b0, b1, b2, s0, s1, c0, c1, weight, place, quant_slots, encoded, terms, window
):
    fill_window(window, (o0, o1, o2), (b0, b1, b2), (s0, s1), (c0, c1), lambda x: x)
    frames, rows, columns, channels = first.shape
    for f in range(frames):
        conv = convolve(window, weight, f).reshape(rows, columns, channels)
        encoded[f] = (first[f].astype(F32) + conv).astype(BF16)
    flat = encoded[...].reshape(frames * rows * columns, channels)
    cells = flat.shape[0]
    slots = quant_slots.shape[0]
    step = 256
    for i in range(slots // step):
        mine = lax.broadcasted_iota(jnp.int32, (step, cells), 0).astype(F32) + float(i * step) == place[0:1, :]
        packed = jnp.dot(onehot(mine), flat, preferred_element_type=F32)
        span = slice(i * step, (i + 1) * step)
        terms[span, :] = (quant_slots[span, :].astype(F32) - packed).astype(BF16)


def quant_kernel(place, *refs):
    parts, quant, quant_slots = refs[:-2], refs[-2], refs[-1]
    cells = quant.shape[0]
    part_slots = parts[0].shape[0]
    column = place[...].T[:, 1:2]
    step = 256
    for i in range(cells // step):
        total = jnp.zeros((step, quant.shape[1]), F32)
        for k, part in enumerate(parts):
            at = lax.broadcasted_iota(jnp.int32, (step, part_slots), 1).astype(F32) + float(k * part_slots)
            mine = onehot(at == column[i * step : (i + 1) * step])
            total = total + jnp.dot(mine, part[...], preferred_element_type=F32)
        quant[i * step : (i + 1) * step, :] = total.astype(BF16)
    rows = quant[...]
    for i in range(quant_slots.shape[0] // step):
        mine = lax.broadcasted_iota(jnp.int32, (step, cells), 0).astype(F32) + float(i * step) == place[0:1, :]
        quant_slots[i * step : (i + 1) * step, :] = jnp.dot(onehot(mine), rows, preferred_element_type=F32).astype(BF16)


def rotate_kernel(encoded, quant, upstream, out):
    step = 128

    def one(i, carry):
        span = pl.ds(pl.multiple_of(i * step, step), step)
        e = encoded[span, :].astype(F32)
        q = quant[span, :].astype(F32)
        g = upstream[span, :].astype(F32)
        lat_norm = jnp.sqrt(jnp.sum(e * e, -1, keepdims=True) + 1e-06)
        quant_norm = jnp.sqrt(jnp.sum(q * q, -1, keepdims=True) + 1e-06)
        a = e / lat_norm
        b = q / quant_norm
        cosine = jnp.sum(a * b, -1, keepdims=True)
        s = a + b
        turned = g - s * (jnp.sum(s * g, -1, keepdims=True) / (1.0 + cosine))
        turned = turned + 2.0 * a * jnp.sum(b * g, -1, keepdims=True)
        out[span, :] = (quant_norm / lat_norm * turned + 2.0 * COMMIT * (e - q)).astype(BF16)
        return carry

    lax.fori_loop(0, encoded.shape[0] // step, one, 0)


def scatter_kernel(target, terms, out):
    rows, slots = out.shape[0], terms.shape[0]
    at = lax.broadcasted_iota(jnp.int32, (rows, slots), 0) + pl.program_id(0) * rows
    sums = jnp.dot(onehot(at == target[...]), terms[...], preferred_element_type=F32)
    out[...] = (2.0 * sums).astype(BF16)


def halo(top, mid, bottom):
    b_top = along(top, "tm", 1)
    b_bottom = along(bottom, "tm", 1)
    up = along(bottom, "height", 1)
    down = along(top, "height", -1)
    b_mid = along(mid, "tm", 1)
    corner_up = along(b_bottom, "height", 1)
    corner_down = along(b_top, "height", -1)
    return b_top, b_mid, b_bottom, up, down, corner_up, corner_down


def on_device(latents, conv_first, conv_second, codebook, codes, upstream):
    frames, rows, columns, channels = latents.shape
    cells = frames * rows * columns
    held = codebook.shape[0]
    tiles = lax.axis_size("tm")
    groups = lax.axis_size("height")
    owners = tiles * groups
    range_rows = held // tiles
    capacity = 2 * cells // owners
    slots = owners * capacity
    block_slots = slots // groups
    video = jax.ShapeDtypeStruct((frames, rows, columns, channels), BF16)
    edge = jax.ShapeDtypeStruct((frames, 1, columns, channels), BF16)
    inner = jax.ShapeDtypeStruct((frames, rows - 2, columns, channels), BF16)

    halo_one = halo(latents[:, :1], latents[:, 1:-1], latents[:, -1:])

    where = lax.axis_index("height").astype(jnp.int32).reshape(1)
    shared = lax.all_gather(codes.reshape(frames * rows, columns), "height")
    ask, low, send, place = pl.pallas_call(
        functools.partial(index_kernel, groups, tiles, held, capacity),
        out_shape=(
            jax.ShapeDtypeStruct((slots // BATCH, BATCH), jnp.int32),
            jax.ShapeDtypeStruct((BATCH, slots // BATCH), F32),
            jax.ShapeDtypeStruct((owners, capacity), jnp.int32),
            jax.ShapeDtypeStruct((8, cells), F32),
        ),
        in_specs=[SMEM, VMEM],
        out_specs=(VMEM,) * 4,
        compiler_params=params(32),
    )(where, shared)
    found = pl.pallas_call(
        functools.partial(gather_kernel, block_slots // BATCH),
        out_shape=(jax.ShapeDtypeStruct((block_slots, channels), BF16),) * groups,
        in_specs=[SMEM, HBM, VMEM],
        out_specs=(VMEM,) * groups,
        scratch_shapes=[
            pltpu.VMEM((slots, TILE, channels), BF16),
            pltpu.SemaphoreType.DMA((slots // BATCH,)),
        ],
        compiler_params=params(40),
    )(ask, codebook.reshape(held // TILE, TILE, channels), low)
    asked = [found[0]] + [around(found[k], "height", k) for k in range(1, groups)]
    owner_codes = lax.all_to_all(send, ("tm", "height"), split_axis=0, concat_axis=0, tiled=True)

    first, top, mid, bottom = pl.pallas_call(
        first_kernel,
        out_shape=(video, edge, inner, edge),
        in_specs=[VMEM] * 9,
        out_specs=(VMEM,) * 4,
        scratch_shapes=[pltpu.VMEM((frames + 2, rows + 2, columns, channels), BF16)],
        compiler_params=params(40),
    )(latents, *halo_one, conv_first)
    halo_two = halo(top, mid, bottom)

    quant, quant_slots = pl.pallas_call(
        quant_kernel,
        out_shape=(
            jax.ShapeDtypeStruct((cells, channels), BF16),
            jax.ShapeDtypeStruct((slots, channels), BF16),
        ),
        in_specs=[VMEM] * (1 + groups),
        out_specs=(VMEM,) * 2,
        compiler_params=params(32),
    )(place, *asked)

    encoded, terms = pl.pallas_call(
        second_kernel,
        out_shape=(video, jax.ShapeDtypeStruct((slots, channels), BF16)),
        in_specs=[VMEM] * 14,
        out_specs=(VMEM,) * 2,
        scratch_shapes=[pltpu.VMEM((frames + 2, rows + 2, columns, channels), BF16)],
        compiler_params=params(40),
    )(first, top, mid, bottom, *halo_two, conv_second, place, quant_slots)
    owner_terms = lax.all_to_all(
        terms.reshape(owners, capacity, channels), ("tm", "height"), split_axis=0, concat_axis=0, tiled=True
    )
    grad_flat = pl.pallas_call(
        rotate_kernel,
        out_shape=jax.ShapeDtypeStruct((cells, channels), BF16),
        in_specs=[VMEM] * 3,
        out_specs=VMEM,
        compiler_params=params(16),
    )(encoded.reshape(cells, channels), quant, upstream.reshape(cells, channels))
    step = 256
    codebook_grad = pl.pallas_call(
        scatter_kernel,
        grid=(range_rows // step,),
        out_shape=jax.ShapeDtypeStruct((range_rows, channels), BF16),
        in_specs=[
            pl.BlockSpec((1, slots), lambda i: (0, 0)),
            pl.BlockSpec((slots, channels), lambda i: (0, 0)),
        ],
        out_specs=pl.BlockSpec((step, channels), lambda i: (i, 0)),
        compiler_params=params(32),
    )(owner_codes.reshape(1, slots), owner_terms.reshape(slots, channels))
    return (grad_flat.reshape(upstream.shape), codebook_grad)


def solution(mesh):
    return jax.shard_map(
        on_device,
        mesh=mesh,
        in_specs=(
            P("tm", "height", None, None),
            P(),
            P(),
            P("height", None),
            P("tm", "height", None),
            P("tm", "height", None, None),
        ),
        out_specs=(P("tm", "height", None, None), P(("height", "tm"), None)),
        check_vma=False,
    )
```

```python
import functools

import jax
import jax.numpy as jnp
from jax import lax
from jax.experimental import pallas as pl
from jax.experimental.pallas import tpu as pltpu
from jax.sharding import PartitionSpec as P

COMMIT = 0.25
BATCH = 64
TILE = 16
BLOCK = 256
F32 = jnp.float32
BF16 = jnp.bfloat16
VMEM = pl.BlockSpec(memory_space=pltpu.VMEM)
SMEM = pl.BlockSpec(memory_space=pltpu.SMEM)
HBM = pl.BlockSpec(memory_space=pltpu.MemorySpace.HBM)
NT = (((1,), (1,)), ((), ()))


def along(x, axis, by):
    count = lax.axis_size(axis)
    return lax.ppermute(x, axis, [(i, i + by) for i in range(count) if 0 <= i + by < count])


def params(megabytes):
    return pltpu.CompilerParams(vmem_limit_bytes=megabytes << 20)


def act(values):
    scaled = values * lax.rsqrt(jnp.mean(values * values, -1, keepdims=True) + 1e-06)
    return scaled / (1.0 + jnp.exp(-scaled))


def lanes(block):
    return jnp.concatenate([block[i : i + 1, :] for i in range(block.shape[0])], axis=1)


def fetch(pairs, sems):
    copies = [pltpu.make_async_copy(src, dst, sems.at[i]) for i, (src, dst) in enumerate(pairs)]
    for copy in copies:
        copy.start()
    return copies


def finish(copies):
    for copy in copies:
        copy.wait()


def onehot(mask):
    return jnp.where(mask, 1.0, 0.0).astype(BF16)


def index_kernel(groups, tiles, held, capacity, where_ref, codes_ref, ask_ref, low_ref, send_ref, place_ref):
    lines, width = codes_ref.shape[1:]
    cells = lines * width
    owners = groups * tiles
    range_rows = held // tiles
    block_slots = tiles * capacity
    batches = block_slots // BATCH
    here = where_ref[0]
    own = lanes(codes_ref[here])
    block = own // range_rows
    target = block % tiles * groups + block // tiles
    home = own // held
    peers = [lanes(codes_ref[k]) for k in range(groups)]
    own_hits = lax.broadcasted_iota(jnp.int32, (owners, cells), 0) == target
    home_hits = lax.broadcasted_iota(jnp.int32, (groups, cells), 0) == home
    peer_hits = [peer // held == here for peer in peers]
    hits = jnp.concatenate(
        [jnp.where(own_hits, 1.0, 0.0), jnp.where(home_hits, 1.0, 0.0)] + [jnp.where(x, 1.0, 0.0) for x in peer_hits], axis=0
    )
    count = hits.shape[0]
    pad = -count % 16
    if pad:
        hits = jnp.concatenate([hits, jnp.zeros((pad, cells), F32)], axis=0)
    earlier = onehot(
        lax.broadcasted_iota(jnp.int32, (width, width), 0) < lax.broadcasted_iota(jnp.int32, (width, width), 1)
    )
    before = jnp.zeros((count + pad, 1), F32)
    parts = []
    for i in range(lines):
        part = hits[:, i * width : (i + 1) * width]
        parts.append(jnp.dot(part.astype(BF16), earlier, preferred_element_type=F32) + before)
        before = before + jnp.sum(part, 1, keepdims=True)
    ranks = jnp.concatenate(parts, axis=1)
    own_rank = jnp.sum(ranks[:owners] * hits[:owners], 0, keepdims=True)
    home_rank = jnp.sum(ranks[owners : owners + groups] * hits[owners : owners + groups], 0, keepdims=True)
    place_ref[0:1, :] = target.astype(F32) * capacity + own_rank
    place_ref[1:2, :] = home.astype(F32) * block_slots + home_rank
    place_ref[2:, :] = jnp.zeros((6, cells), F32)
    local = own % range_rows
    own_ones = hits[:owners]
    picked = jnp.concatenate(
        [own_ones * (local // 256).astype(F32), own_ones * (local % 256).astype(F32), own_ones], axis=0
    ).astype(BF16)
    chosen = onehot(lax.broadcasted_iota(jnp.int32, (capacity, cells), 0).astype(F32) == own_rank)
    slots = lax.dot_general(picked, chosen, NT, preferred_element_type=F32)
    code = slots[:owners] * 256.0 + slots[owners : 2 * owners]
    send_ref[...] = jnp.where(slots[2 * owners :] > 0.5, code, -1.0).astype(jnp.int32)
    columns = []
    for k in range(groups):
        hit = hits[owners + groups + k : owners + groups + k + 1]
        rank = ranks[owners + groups + k : owners + groups + k + 1].astype(jnp.int32)
        row = jnp.where(peer_hits[k], peers[k] - here * held, 0)
        batch = onehot(
            lax.broadcasted_iota(jnp.int32, (batches, cells), 0) == jnp.where(peer_hits[k], rank // BATCH, -1)
        ).astype(F32)
        tile = row // TILE
        picked = jnp.concatenate(
            [
                batch * (tile // 128).astype(F32),
                batch * (tile % 128).astype(F32),
                batch,
                batch * (row % TILE).astype(F32),
            ],
            axis=0,
        ).astype(BF16)
        chosen = onehot(lax.broadcasted_iota(jnp.int32, (BATCH, cells), 0) == rank % BATCH)
        slots = lax.dot_general(picked, chosen, NT, preferred_element_type=F32)
        asked = slots[:batches] * 128.0 + slots[batches : 2 * batches]
        ask_ref[k * batches : (k + 1) * batches, :] = jnp.where(
            slots[2 * batches : 3 * batches] > 0.5, asked, -1.0
        ).astype(jnp.int32)
        columns.append(lax.dot_general(chosen, picked[3 * batches :], NT, preferred_element_type=F32))
    low_ref[...] = jnp.concatenate(columns, axis=1)


def gather_kernel(ask_ref, book_ref, low_ref, out_ref, land, out, sems, out_sem):
    total = out.shape[0] // BATCH

    def copy_in(g):
        def one(i, carry):
            tile = jnp.maximum(ask_ref[g, i], 0)
            pltpu.make_async_copy(book_ref.at[tile], land.at[g * BATCH + i], sems.at[g]).start()
            return carry

        lax.fori_loop(0, BATCH, one, 0, unroll=16)

    for g in range(total):
        pl.when(ask_ref[g, 0] >= 0)(functools.partial(copy_in, g))
    at = lax.broadcasted_iota(jnp.int32, (BATCH, BATCH * TILE), 1)
    at = at - TILE * lax.broadcasted_iota(jnp.int32, (BATCH, BATCH * TILE), 0)
    at = at.astype(F32)
    for g in range(total):
        span = slice(g * BATCH, (g + 1) * BATCH)
        filled = ask_ref[g, 0] >= 0

        @pl.when(filled)
        def _(g=g, span=span):
            block = land.at[pl.ds(g * BATCH, BATCH)]
            pltpu.make_async_copy(book_ref.at[pl.ds(0, BATCH)], block, sems.at[g]).wait()
            tiles = land[span].reshape(BATCH * TILE, land.shape[-1])
            out[span, :] = jnp.dot(onehot(at == low_ref[:, g : g + 1]), tiles, preferred_element_type=F32).astype(BF16)

        @pl.when(jnp.logical_not(filled))
        def _(span=span):
            out[span, :] = jnp.zeros((BATCH, out.shape[-1]), BF16)

    finish(fetch([(out, out_ref)], out_sem))


def split_kernel(video, edges, inner, sems):
    rows = video.shape[1]
    finish(
        fetch(
            [
                (video.at[:, pl.ds(0, 1)], edges.at[:, pl.ds(0, 1)]),
                (video.at[:, pl.ds(rows - 1, 1)], edges.at[:, pl.ds(1, 1)]),
                (video.at[:, pl.ds(1, rows - 2)], inner),
            ],
            sems,
        )
    )


def join_kernel(before, own, top, bottom, sems):
    frames = own.shape[0]
    old, new = pl.ds(0, frames), pl.ds(frames, frames)
    finish(
        fetch(
            [
                (before.at[:, pl.ds(0, 1)], top.at[old]),
                (own.at[:, pl.ds(0, 1)], top.at[new]),
                (before.at[:, pl.ds(1, 1)], bottom.at[old]),
                (own.at[:, pl.ds(1, 1)], bottom.at[new]),
            ],
            sems,
        )
    )


def taps(patch, weight, columns):
    flat = patch.shape[0]
    place = lax.broadcasted_iota(jnp.int32, (flat, 1), 0) % columns
    sums = [jnp.dot(patch, weight(r), preferred_element_type=F32) for r in range(3)]
    left = jnp.where(place == 0, 0.0, pltpu.roll(sums[0], 1, 0))
    right = jnp.where(place == columns - 1, 0.0, pltpu.roll(sums[2], flat - 1, 0))
    return sums[1] + left + right


def frame_taps(window, weight, out, early, late):
    rows, columns, channels = window.shape[1] - 2, window.shape[2], window.shape[3]
    pieces = [
        window[f, q : q + rows].reshape(rows * columns, channels) for f in range(early, late) for q in range(3)
    ]
    size = len(pieces) * channels
    return taps(
        jnp.concatenate(pieces, axis=1),
        lambda r: weight[early - out : late - out, :, r].reshape(size, channels),
        columns,
    )


def edge_taps(window, weight, out, side):
    columns, channels = window.shape[2], window.shape[3]
    row, q = (0, 0) if side == 0 else (window.shape[1] - 1, 2)
    last = out + 3
    pieces = [window[f, row] for f in range(2, last)]
    size = len(pieces) * channels
    return taps(
        jnp.concatenate(pieces, axis=1),
        lambda r: weight[2 - out : 3, q, r].reshape(size, channels),
        columns,
    )


def activate(ref):
    ref[...] = act(ref[...].astype(F32)).astype(BF16)


def own_first_kernel(video, weight, partial, window, source, result, sems):
    frames, rows, columns, channels = source.shape
    copies = fetch([(video, source)], sems)
    window[2:4, 0:1] = jnp.zeros((frames, 1, columns, channels), BF16)
    window[2:4, rows + 1 :] = jnp.zeros((frames, 1, columns, channels), BF16)
    finish(copies)
    outs = []
    for f in range(frames):
        window[2 + f, 1 : rows + 1] = act(source[f].astype(F32)).astype(BF16)
        added = frame_taps(window, weight, f, 2, f + 3)
        result[f] = source[f].astype(F32) + added.reshape(rows, columns, channels)
        outs.append(pltpu.make_async_copy(result.at[f], partial.at[f], sems.at[1 + f]))
        outs[-1].start()
    finish(outs)


def own_second_kernel(first, edges, inner, weight, partial, window, source, result, sems):
    frames, rows, columns, channels = source.shape
    new = pl.ds(2, frames)
    copies = fetch(
        [
            (edges.at[:, pl.ds(0, 1)], window.at[new, pl.ds(1, 1)]),
            (inner, window.at[new, pl.ds(2, rows - 2)]),
            (edges.at[:, pl.ds(1, 1)], window.at[new, pl.ds(rows, 1)]),
            (first, source),
        ],
        sems,
    )
    window[2:4, 0:1] = jnp.zeros((frames, 1, columns, channels), BF16)
    window[2:4, rows + 1 :] = jnp.zeros((frames, 1, columns, channels), BF16)
    finish(copies)
    outs = []
    for f in range(frames):
        added = frame_taps(window, weight, f, 2, f + 3)
        result[f] = source[f].astype(F32) + added.reshape(rows, columns, channels)
        outs.append(pltpu.make_async_copy(result.at[f], partial.at[f], sems.at[4 + f]))
        outs[-1].start()
    finish(outs)


def fill(edges, inner, up, down, partial, window, total, sems):
    frames, rows = total.shape[0], total.shape[1]
    old = pl.ds(0, frames)
    return fetch(
        [
            (edges.at[:, pl.ds(0, 1)], window.at[old, pl.ds(1, 1)]),
            (edges.at[:, pl.ds(1, 1)], window.at[old, pl.ds(rows, 1)]),
            (inner, window.at[old, pl.ds(2, rows - 2)]),
            (up, window.at[:, pl.ds(0, 1)]),
            (down, window.at[:, pl.ds(rows + 1, 1)]),
            (partial, total),
        ],
        sems,
    )


def rest(window, weight, total, f):
    frames, rows, columns, channels = total.shape
    full = total[f] + frame_taps(window, weight, f, f, 2).reshape(rows, columns, channels)
    return (
        full[0:1] + edge_taps(window, weight, f, 0).reshape(1, columns, channels),
        full[1:-1],
        full[-1:] + edge_taps(window, weight, f, 1).reshape(1, columns, channels),
    )


def first_kernel(edges, inner, up, down, partial, weight, first, top2, inner2, window, total, a, b, c, sems):
    frames, rows, columns, channels = total.shape
    finish(fill(edges, inner, up, down, partial, window, total, sems))
    for f in range(frames):
        activate(window.at[f])
    for f in range(frames):
        activate(window.at[2 + f, pl.ds(0, 1)])
        activate(window.at[2 + f, pl.ds(rows + 1, 1)])
    outs = []
    for f in range(frames):
        top, middle, bottom = rest(window, weight, total, f)
        a[f, 0:1] = top.astype(BF16)
        a[f, 1:-1] = middle.astype(BF16)
        a[f, -1:] = bottom.astype(BF16)
        active = act(a[f].astype(F32)).astype(BF16)
        b[f, 0:1] = active[0:1]
        b[f, 1:2] = active[-1:]
        c[f] = active[1:-1]
        for i, (src, dst) in enumerate(((b, top2), (c, inner2), (a, first))):
            outs.append(pltpu.make_async_copy(src.at[f], dst.at[f], sems.at[6 + 3 * f + i]))
            outs[-1].start()
    finish(outs)


def second_kernel(edges, inner, up, down, partial, weight, place, encoded, terms, window, total, a, packed, sems):
    frames, rows, columns, channels = total.shape
    finish(fill(edges, inner, up, down, partial, window, total, sems))
    outs = []
    for f in range(frames):
        top, middle, bottom = rest(window, weight, total, f)
        a[f, 0:1] = top.astype(BF16)
        a[f, 1:-1] = middle.astype(BF16)
        a[f, -1:] = bottom.astype(BF16)
        outs.append(pltpu.make_async_copy(a.at[f], encoded.at[f], sems.at[6 + f]))
        outs[-1].start()
    flat = a[...].reshape(frames * rows * columns, channels)
    cells = flat.shape[0]
    step = 256
    for i in range(packed.shape[0] // step):
        mine = lax.broadcasted_iota(jnp.int32, (step, cells), 0).astype(F32) + float(i * step) == place[0:1, :]
        span = pl.ds(i * step, step)
        packed[span, :] = jnp.dot(onehot(mine), flat, preferred_element_type=F32).astype(BF16)
        outs.append(pltpu.make_async_copy(packed.at[span], terms.at[span], sems.at[6 + frames + i]))
        outs[-1].start()
    finish(outs)


def rotate_kernel(place, found, encoded, upstream, grad, rows_in, e_in, g_in, out, sems):
    copies = fetch([(found, rows_in), (encoded, e_in), (upstream, g_in)], sems)
    cells, slots = out.shape[0], rows_in.shape[0]
    column = place[...].T[:, 1:2]
    finish(copies)
    step = 256
    for i in range(cells // step):
        span = slice(i * step, (i + 1) * step)
        mine = onehot(lax.broadcasted_iota(jnp.int32, (step, slots), 1).astype(F32) == column[span])
        q = jnp.dot(mine, rows_in[...], preferred_element_type=F32)
        e = e_in[span, :].astype(F32)
        g = g_in[span, :].astype(F32)
        lat_norm = jnp.sqrt(jnp.sum(e * e, -1, keepdims=True) + 1e-06)
        quant_norm = jnp.sqrt(jnp.sum(q * q, -1, keepdims=True) + 1e-06)
        a = e / lat_norm
        b = q / quant_norm
        cosine = jnp.sum(a * b, -1, keepdims=True)
        s = a + b
        turned = g - s * (jnp.sum(s * g, -1, keepdims=True) / (1.0 + cosine))
        turned = turned + 2.0 * a * jnp.sum(b * g, -1, keepdims=True)
        out[span, :] = (quant_norm / lat_norm * turned + 2.0 * COMMIT * (e - q)).astype(BF16)
    finish(fetch([(out, grad)], sems))


def sort_kernel(code_ref, bounds_ref, order_ref, sorted_ref):
    slots = code_ref.shape[1]
    blocks = bounds_ref.shape[0]
    chunks = slots // BLOCK
    width = 128
    code = code_ref[...]
    block = jnp.where(code >= 0, code // BLOCK, -1)
    hits = jnp.where(lax.broadcasted_iota(jnp.int32, (blocks, slots), 0) == block, 1.0, 0.0)
    earlier = onehot(
        lax.broadcasted_iota(jnp.int32, (width, width), 0) < lax.broadcasted_iota(jnp.int32, (width, width), 1)
    )
    before = jnp.zeros((blocks, 1), F32)
    parts = []
    for i in range(slots // width):
        part = hits[:, i * width : (i + 1) * width]
        parts.append(jnp.dot(part.astype(BF16), earlier, preferred_element_type=F32) + before)
        before = before + jnp.sum(part, 1, keepdims=True)
    ranks = jnp.concatenate(parts, axis=1)
    counts = lax.dot_general(jnp.ones((8, slots), BF16), hits.astype(BF16), NT, preferred_element_type=F32)[0:1]
    lower = lax.broadcasted_iota(jnp.int32, (blocks, blocks), 1) < lax.broadcasted_iota(jnp.int32, (blocks, blocks), 0)
    starts = jnp.sum(jnp.where(lower, counts, 0.0), 1, keepdims=True)
    lane = lax.broadcasted_iota(jnp.int32, (blocks, width), 1)
    bounds_ref[...] = jnp.where(lane == 0, starts, starts + before).astype(jnp.int32)
    order = jnp.sum(hits * (ranks + starts), 0, keepdims=True)
    order = jnp.where(code >= 0, order, -1.0)
    order_ref[...] = order
    at = order.astype(jnp.int32)
    chunk = lax.broadcasted_iota(jnp.int32, (chunks, slots), 0) == jnp.where(at >= 0, at // BLOCK, -1)
    ones = jnp.where(chunk, 1.0, 0.0)
    picked = jnp.concatenate(
        [ones * (code // BLOCK).astype(F32), ones * (code % BLOCK).astype(F32), ones], axis=0
    ).astype(BF16)
    chosen = onehot(lax.broadcasted_iota(jnp.int32, (BLOCK, slots), 0) == at % BLOCK)
    spread = lax.dot_general(picked, chosen, NT, preferred_element_type=F32)
    inside = jnp.where(
        spread[2 * chunks :] > 0.5, spread[:chunks] * float(BLOCK) + spread[chunks : 2 * chunks], -1.0
    )
    sorted_ref[...] = jnp.full(sorted_ref.shape, -1, jnp.int32)
    sorted_ref[:chunks, :] = inside.astype(jnp.int32)


def scatter_kernel(bounds, shard, terms, book, order, codes, grad, rows_in, book_in, ranked, out, sums, sems):
    slots = rows_in.shape[0]
    chunks = slots // BLOCK
    blocks = out.shape[0] // BLOCK
    own = pl.ds(pl.multiple_of(shard[0] * out.shape[0], BLOCK), out.shape[0])
    copies = fetch([(terms, rows_in), (book.at[own], book_in)], sems)
    copies[0].wait()
    for i in range(chunks):
        mine = lax.broadcasted_iota(jnp.int32, (BLOCK, slots), 0).astype(F32) + float(i * BLOCK) == order[...]
        ranked[i * BLOCK : (i + 1) * BLOCK, :] = jnp.dot(
            onehot(mine), rows_in[...], preferred_element_type=F32
        ).astype(BF16)
    ranked[slots:, :] = jnp.zeros((ranked.shape[0] - slots, ranked.shape[1]), BF16)
    copies[1].wait()
    at = lax.broadcasted_iota(jnp.int32, (BLOCK, BLOCK), 0)
    outs = []
    for b in range(blocks):
        first = bounds[b, 0] // BLOCK
        after = (bounds[b, 1] + BLOCK - 1) // BLOCK

        def part(j, b=b):
            mine = jnp.where(at + b * BLOCK == codes[pl.ds(j, 1), :], 1.0, 0.0)
            rows = ranked[pl.ds(pl.multiple_of(j * BLOCK, BLOCK), BLOCK), :]
            total = jnp.dot(mine.astype(BF16), rows, preferred_element_type=F32)
            return jnp.sum(mine, 1, keepdims=True) * book_in[b * BLOCK : (b + 1) * BLOCK, :].astype(F32) - total

        span = pl.ds(b * BLOCK, BLOCK)
        out[span, :] = (2.0 * (part(first) + part(first + 1))).astype(BF16)

        @pl.when(after > first + 2)
        def _(first=first, after=after, part=part, span=span):
            sums[...] = part(first) + part(first + 1)

            def more(j, carry):
                sums[...] += part(j)
                return carry

            lax.fori_loop(first + 2, after, more, 0)
            out[span, :] = (2.0 * sums[...]).astype(BF16)

        outs.append(pltpu.make_async_copy(out.at[span], grad.at[span], sems.at[2 + b]))
        outs[-1].start()
    finish(outs)


def shape(dims, dtype=BF16):
    return jax.ShapeDtypeStruct(tuple(dims), dtype)


def halo(edges, inner):
    old_edges = along(edges, "tm", 1)
    old_inner = along(inner, "tm", 1)
    frames, _, columns, channels = edges.shape
    both = shape((2 * frames, 1, columns, channels))
    top, bottom = pl.pallas_call(
        join_kernel,
        out_shape=(both, both),
        in_specs=[HBM] * 2,
        out_specs=(HBM,) * 2,
        scratch_shapes=[pltpu.SemaphoreType.DMA((4,))],
        compiler_params=params(8),
    )(old_edges, edges)
    return old_edges, old_inner, along(bottom, "height", 1), along(top, "height", -1)


def on_device(latents, conv_first, conv_second, codebook, codes, upstream):
    frames, rows, columns, channels = latents.shape
    cells = frames * rows * columns
    held = codebook.shape[0]
    tiles = lax.axis_size("tm")
    groups = lax.axis_size("height")
    owners = tiles * groups
    range_rows = held // tiles
    capacity = 2 * cells // owners
    slots = owners * capacity
    block = (frames, rows, columns, channels)
    pair = (frames, 2, columns, channels)
    middle = (frames, rows - 2, columns, channels)
    window = pltpu.VMEM((frames + 2, rows + 2, columns, channels), BF16)
    sems = pltpu.SemaphoreType.DMA

    edges, inner = pl.pallas_call(
        split_kernel,
        out_shape=(shape(pair), shape(middle)),
        in_specs=[HBM],
        out_specs=(HBM,) * 2,
        scratch_shapes=[sems((3,))],
        compiler_params=params(8),
    )(latents)
    halo_one = halo(edges, inner)

    where = lax.axis_index("height").astype(jnp.int32).reshape(1)
    shard = lax.axis_index("tm").astype(jnp.int32).reshape(1)
    shared = lax.all_gather(codes.reshape(frames * rows, columns), "height")
    ask, low, send, place = pl.pallas_call(
        functools.partial(index_kernel, groups, tiles, held, capacity),
        out_shape=(
            shape((slots // BATCH, BATCH), jnp.int32),
            shape((BATCH, slots // BATCH), F32),
            shape((owners, capacity), jnp.int32),
            shape((8, cells), F32),
        ),
        in_specs=[SMEM, VMEM],
        out_specs=(VMEM,) * 4,
        compiler_params=params(24),
    )(where, shared)

    partial_one = pl.pallas_call(
        own_first_kernel,
        out_shape=shape(block, F32),
        in_specs=[HBM, VMEM],
        out_specs=HBM,
        scratch_shapes=[window, pltpu.VMEM(block, BF16), pltpu.VMEM(block, F32), sems((1 + frames,))],
        compiler_params=params(24),
    )(latents, conv_first)
    first, edges, inner = pl.pallas_call(
        first_kernel,
        out_shape=(shape(block), shape(pair), shape(middle)),
        in_specs=[HBM] * 5 + [VMEM],
        out_specs=(HBM,) * 3,
        scratch_shapes=[
            window,
            pltpu.VMEM(block, F32),
            pltpu.VMEM(block, BF16),
            pltpu.VMEM(pair, BF16),
            pltpu.VMEM(middle, BF16),
            sems((6 + 3 * frames,)),
        ],
        compiler_params=params(24),
    )(*halo_one, partial_one, conv_first)
    halo_two = halo(edges, inner)

    found = pl.pallas_call(
        gather_kernel,
        out_shape=shape((slots, channels)),
        in_specs=[SMEM, HBM, VMEM],
        out_specs=HBM,
        scratch_shapes=[
            pltpu.VMEM((slots, TILE, channels), BF16),
            pltpu.VMEM((slots, channels), BF16),
            sems((slots // BATCH,)),
            sems((1,)),
        ],
        compiler_params=params(32),
    )(ask, codebook.reshape(held // TILE, TILE, channels), low)
    found = lax.all_to_all(
        found.reshape(groups, slots // groups, channels), "height", split_axis=0, concat_axis=0, tiled=True
    )
    owner_codes = lax.all_to_all(send, ("tm", "height"), split_axis=0, concat_axis=0, tiled=True)

    partial_two = pl.pallas_call(
        own_second_kernel,
        out_shape=shape(block, F32),
        in_specs=[HBM] * 3 + [VMEM],
        out_specs=HBM,
        scratch_shapes=[window, pltpu.VMEM(block, BF16), pltpu.VMEM(block, F32), sems((4 + frames,))],
        compiler_params=params(24),
    )(first, edges, inner, conv_second)
    encoded, terms = pl.pallas_call(
        second_kernel,
        out_shape=(shape(block), shape((slots, channels))),
        in_specs=[HBM] * 5 + [VMEM] * 2,
        out_specs=(HBM,) * 2,
        scratch_shapes=[
            window,
            pltpu.VMEM(block, F32),
            pltpu.VMEM(block, BF16),
            pltpu.VMEM((slots, channels), BF16),
            sems((6 + frames + slots // 256,)),
        ],
        compiler_params=params(24),
    )(*halo_two, partial_two, conv_second, place)
    owner_terms = lax.all_to_all(
        terms.reshape(owners, capacity, channels), ("tm", "height"), split_axis=0, concat_axis=0, tiled=True
    )

    blocks = range_rows // BLOCK
    chunks = slots // BLOCK
    bounds, order, ranked = pl.pallas_call(
        sort_kernel,
        out_shape=(
            shape((blocks, 128), jnp.int32),
            shape((1, slots), F32),
            shape((-(-(chunks + 2) // 8) * 8, BLOCK), jnp.int32),
        ),
        in_specs=[VMEM],
        out_specs=(VMEM,) * 3,
        compiler_params=params(24),
    )(owner_codes.reshape(1, slots))
    grad = pl.pallas_call(
        rotate_kernel,
        out_shape=shape((cells, channels)),
        in_specs=[VMEM] + [HBM] * 3,
        out_specs=HBM,
        scratch_shapes=[pltpu.VMEM((slots, channels), BF16)] + [pltpu.VMEM((cells, channels), BF16)] * 3 + [sems((3,))],
        compiler_params=params(24),
    )(
        place,
        found.reshape(slots, channels),
        encoded.reshape(cells, channels),
        upstream.reshape(cells, channels),
    )
    codebook_grad = pl.pallas_call(
        scatter_kernel,
        out_shape=shape((range_rows, channels)),
        in_specs=[SMEM, SMEM, HBM, HBM, VMEM, VMEM],
        out_specs=HBM,
        scratch_shapes=[
            pltpu.VMEM((slots, channels), BF16),
            pltpu.VMEM((range_rows, channels), BF16),
            pltpu.VMEM((slots + 2 * BLOCK, channels), BF16),
            pltpu.VMEM((range_rows, channels), BF16),
            pltpu.VMEM((BLOCK, channels), F32),
            sems((2 + blocks,)),
        ],
        compiler_params=params(32),
    )(bounds, shard, owner_terms.reshape(slots, channels), codebook, order, ranked)
    return (grad.reshape(upstream.shape), codebook_grad)


def solution(mesh):
    return jax.shard_map(
        on_device,
        mesh=mesh,
        in_specs=(
            P("tm", "height", None, None),
            P(),
            P(),
            P("height", None),
            P("tm", "height", None),
            P("tm", "height", None, None),
        ),
        out_specs=(P("tm", "height", None, None), P(("height", "tm"), None)),
        check_vma=False,
    )
```

```python
import functools

import jax
import jax.numpy as jnp
from jax import lax
from jax.experimental import pallas as pl
from jax.experimental.pallas import tpu as pltpu
from jax.sharding import PartitionSpec as P

COMMIT = 0.25
BATCH = 64
TILE = 16
BLOCK = 256
F32 = jnp.float32
BF16 = jnp.bfloat16
VMEM = pl.BlockSpec(memory_space=pltpu.VMEM)
SMEM = pl.BlockSpec(memory_space=pltpu.SMEM)
HBM = pl.BlockSpec(memory_space=pltpu.MemorySpace.HBM)
NT = (((1,), (1,)), ((), ()))


def along(x, axis, by):
    count = lax.axis_size(axis)
    return lax.ppermute(x, axis, [(i, i + by) for i in range(count) if 0 <= i + by < count])


def around(x, axis, by):
    count = lax.axis_size(axis)
    return lax.ppermute(x, axis, [(i, (i + by) % count) for i in range(count)])


def params(megabytes=28):
    return pltpu.CompilerParams(vmem_limit_bytes=megabytes << 20)


def act(values):
    scaled = values * lax.rsqrt(jnp.mean(values * values, -1, keepdims=True) + 1e-06)
    return scaled / (1.0 + jnp.exp(-scaled))


def lanes(block):
    return jnp.concatenate([block[i : i + 1, :] for i in range(block.shape[0])], axis=1)


def fetch(pairs, sems):
    copies = [pltpu.make_async_copy(src, dst, sems.at[i]) for i, (src, dst) in enumerate(pairs)]
    for copy in copies:
        copy.start()
    return copies


def finish(copies):
    for copy in copies:
        copy.wait()


def onehot(mask):
    return jnp.where(mask, 1.0, 0.0).astype(BF16)


def index_kernel(groups, tiles, held, capacity, here_ref, codes_ref, send_ref, place_ref):
    lines, width = codes_ref.shape
    cells = lines * width
    owners = groups * tiles
    range_rows = held // tiles
    block_slots = tiles * capacity
    near, here = here_ref[0], here_ref[1]
    own = lanes(codes_ref[...])
    block = own // range_rows
    target = block % tiles * groups + block // tiles
    home = own // held
    own_hits = lax.broadcasted_iota(jnp.int32, (owners, cells), 0) == target
    home_hits = lax.broadcasted_iota(jnp.int32, (groups, cells), 0) == home
    pad = -(owners + groups) % 16
    hits = jnp.concatenate(
        [jnp.where(own_hits, 1.0, 0.0), jnp.where(home_hits, 1.0, 0.0), jnp.zeros((pad, cells), F32)], axis=0
    )
    earlier = onehot(
        lax.broadcasted_iota(jnp.int32, (width, width), 0) < lax.broadcasted_iota(jnp.int32, (width, width), 1)
    )
    before = jnp.zeros((hits.shape[0], 1), F32)
    parts = []
    for i in range(lines):
        part = hits[:, i * width : (i + 1) * width]
        parts.append(jnp.dot(part.astype(BF16), earlier, preferred_element_type=F32) + before)
        before = before + jnp.sum(part, 1, keepdims=True)
    ranks = hits * jnp.concatenate(parts, axis=1)
    own_rank = jnp.sum(ranks[:owners], 0, keepdims=True)
    home_rank = jnp.sum(ranks[owners : owners + groups], 0, keepdims=True)
    arrival = lax.rem(here - home + groups, groups)
    place_ref[0:1, :] = target.astype(F32) * capacity + own_rank
    place_ref[1:2, :] = arrival.astype(F32) * block_slots + home_rank
    place_ref[2:, :] = jnp.zeros((6, cells), F32)
    send_ref[...] = jnp.zeros(send_ref.shape, jnp.int32)

    def spread(ones, code, rank):
        count = ones.shape[0]
        high, low = (code // 256).astype(F32), (code % 256).astype(F32)
        picked = jnp.concatenate([ones * high, ones * low, ones], axis=0).astype(BF16)
        chosen = onehot(lax.broadcasted_iota(jnp.int32, (width, cells), 0) == rank)
        out = lax.dot_general(picked, chosen, NT, preferred_element_type=F32)
        code = out[:count] * 256.0 + out[count : 2 * count]
        return jnp.where(out[2 * count :] > 0.5, code, -1.0).astype(jnp.int32)

    send_ref[:, 7, :] = spread(hits[:owners], own % range_rows, own_rank.astype(jnp.int32))
    asked_lines = block_slots // width
    line = home_rank.astype(jnp.int32) // width
    for h in range(groups):
        ones = jnp.where(
            (lax.broadcasted_iota(jnp.int32, (8, cells), 0) == line) & (home == h), 1.0, 0.0
        )
        asked = spread(ones, own % held, home_rank.astype(jnp.int32) % width)
        send_ref[near * groups + h, 0:asked_lines, :] = asked[:asked_lines]


def gather_kernel(groups, here_ref, asked_ref, book_ref, _, *refs):
    outs, (done, ask, lows, land, out, sems, out_sems) = refs[:groups], refs[groups:]
    done[...] = jnp.zeros_like(done)
    rows, width = ask.shape
    near, here = here_ref[0], here_ref[1]
    mine = asked_ref.at[pl.ds(pl.multiple_of(near * rows, 8), rows)]
    finish(fetch([(mine, ask), (mine, lows)], out_sems))
    total = out.shape[0] // BATCH
    size = out.shape[0] // groups

    def spot(g):
        peer, inside = divmod(g * BATCH, size)
        return peer * (rows // groups) + inside // width, inside % width

    def copy_in(g):
        line, first = spot(g)

        def one(i, carry):
            tile = jnp.maximum(ask[line, first + i], 0) // TILE
            pltpu.make_async_copy(book_ref.at[tile], land.at[g * BATCH + i], sems.at[g]).start()
            return carry

        lax.fori_loop(0, BATCH, one, 0, unroll=16)

    for g in range(total):
        pl.when(ask[spot(g)] >= 0)(functools.partial(copy_in, g))
    low = jnp.concatenate([(lows[...] % TILE).astype(F32), jnp.zeros((width - rows, width), F32)], axis=0).T
    at = lax.broadcasted_iota(jnp.int32, (BATCH, BATCH * TILE), 1)
    at = at - TILE * lax.broadcasted_iota(jnp.int32, (BATCH, BATCH * TILE), 0)
    at = at.astype(F32)
    for g in range(total):
        span = slice(g * BATCH, (g + 1) * BATCH)
        line, first = spot(g)
        filled = ask[line, first] >= 0

        @pl.when(filled)
        def _(g=g, span=span, line=line, first=first):
            block = land.at[pl.ds(g * BATCH, BATCH)]
            pltpu.make_async_copy(book_ref.at[pl.ds(0, BATCH)], block, sems.at[g]).wait()
            tiles = land[span].reshape(BATCH * TILE, land.shape[-1])
            wanted = onehot(at == low[first : first + BATCH, line : line + 1])
            out[span, :] = jnp.dot(wanted, tiles, preferred_element_type=F32).astype(BF16)

        @pl.when(jnp.logical_not(filled))
        def _(span=span):
            out[span, :] = jnp.zeros((BATCH, out.shape[-1]), BF16)

    parts = []
    for k in range(groups):
        peer = lax.rem(here + k, groups)
        parts.append((out.at[pl.ds(pl.multiple_of(peer * size, BATCH), size)], outs[k]))
    finish(fetch(parts, out_sems))


def join_kernel(before, own, _, _asked, top, bottom, held, sems):
    frames, rows = own.shape[:2]
    old, new = pl.ds(0, frames), pl.ds(frames, frames)
    first, last = pl.ds(0, 1), pl.ds(rows - 1, 1)
    ins = fetch(
        [
            (before.at[:, first], held.at[0, old]),
            (own.at[:, first], held.at[0, new]),
            (before.at[:, last], held.at[1, old]),
            (own.at[:, last], held.at[1, new]),
        ],
        sems,
    )
    finish(ins[2:])
    outs = fetch([(held.at[1], bottom)], sems.at[pl.ds(4, 1)])
    finish(ins[:2])
    outs += fetch([(held.at[0], top)], sems.at[pl.ds(5, 1)])
    finish(outs)


def taps(patch, weight, columns):
    flat = patch.shape[0]
    place = lax.broadcasted_iota(jnp.int32, (flat, 1), 0) % columns
    sums = [jnp.dot(patch, weight(r), preferred_element_type=F32) for r in range(3)]
    left = jnp.where(place == 0, 0.0, pltpu.roll(sums[0], 1, 0))
    right = jnp.where(place == columns - 1, 0.0, pltpu.roll(sums[2], flat - 1, 0))
    return sums[1] + left + right


def frame_taps(window, weight, frame, count, t):
    rows, columns, channels = window.shape[1] - 2, window.shape[2], window.shape[3]
    pieces = [
        window[frame : frame + count, q : q + rows].reshape(count * rows * columns, channels) for q in range(3)
    ]
    return taps(
        jnp.concatenate(pieces, axis=1), lambda r: weight[t, :, r].reshape(3 * channels, channels), columns
    ).reshape(count, rows, columns, channels)


def edge_taps(window, weight, side):
    columns, channels = window.shape[2], window.shape[3]
    row, q = (0, 0) if side == 0 else (window.shape[1] - 1, 2)
    one, two = window[2, row], window[3, row]
    before = jnp.concatenate([jnp.zeros_like(one), one], axis=0)
    patch = jnp.concatenate([before, jnp.concatenate([one, two], axis=0)], axis=1)
    return taps(
        patch, lambda r: weight[1:, q, r].reshape(2 * channels, channels), columns
    ).reshape(2, 1, columns, channels)


def own_kernel(change, own, residual, weight, _, partial, done, window, source, result, sems):
    frames, rows, columns, channels = source.shape
    copies = fetch([(own, window.at[pl.ds(2, frames), pl.ds(1, rows)]), (residual, source)], sems)
    empty = jnp.zeros((frames, 1, columns, channels), BF16)
    window[2:, 0:1] = empty
    window[2:, rows + 1 :] = empty
    done[...] = jnp.zeros_like(done)
    copies[0].wait()
    if change:
        for f in range(2, frames + 2):
            window[f, 1 : rows + 1] = act(window[f, 1 : rows + 1].astype(F32)).astype(BF16)
    copies[1].wait()
    result[...] = source[...].astype(F32) + frame_taps(window, weight, 2, 2, 2)
    first = fetch([(result.at[0], partial.at[0])], sems.at[pl.ds(2, 1)])
    result[1] += frame_taps(window, weight, 2, 1, 1)[0]
    finish(first + fetch([(result.at[1], partial.at[1])], sems.at[pl.ds(3, 1)]))


def rest(change, before, up, down, partial, weight, window, total, sems):
    frames, rows, columns, channels = total.shape
    copies = fetch(
        [
            (before, window.at[pl.ds(0, 2), pl.ds(1, rows)]),
            (up, window.at[:, pl.ds(0, 1)]),
            (down, window.at[:, pl.ds(rows + 1, 1)]),
            (partial, total),
        ],
        sems,
    )
    finish(copies[:3])
    if change:
        for f in range(frames + 2):
            for span in (slice(0, rows + 2),) if f < 2 else (slice(0, 1), slice(rows + 1, rows + 2)):
                window[f, span] = act(window[f, span].astype(F32)).astype(BF16)
    copies[3].wait()
    total[...] += frame_taps(window, weight, 0, 2, 0)
    total[0:1] += frame_taps(window, weight, 1, 1, 1)
    total[:, 0:1] += edge_taps(window, weight, 0)
    total[:, -1:] += edge_taps(window, weight, 1)


def first_kernel(before, up, down, partial, weight, first, active, done, window, total, a, b, sems):
    done[...] = jnp.zeros_like(done)
    rest(True, before, up, down, partial, weight, window, total, sems)
    outs = []
    for f in range(total.shape[0]):
        a[f] = total[f].astype(BF16)
        b[f] = act(a[f].astype(F32)).astype(BF16)
        for i, (src, dst) in enumerate(((b, active), (a, first))):
            outs.append(pltpu.make_async_copy(src.at[f], dst.at[f], sems.at[4 + 2 * f + i]))
            outs[-1].start()
    finish(outs)


def second_kernel(before, up, down, partial, weight, place, encoded, terms, window, total, a, packed, sems):
    rest(False, before, up, down, partial, weight, window, total, sems)
    frames, rows, columns, channels = total.shape
    a[...] = total[...].astype(BF16)
    outs = fetch([(a, encoded)], sems.at[pl.ds(4, 1)])
    flat = a[...].reshape(frames * rows * columns, channels)
    cells = flat.shape[0]
    step = 256
    for i in range(packed.shape[0] // step):
        mine = lax.broadcasted_iota(jnp.int32, (step, cells), 0).astype(F32) + float(i * step) == place[0:1, :]
        span = pl.ds(i * step, step)
        packed[span, :] = jnp.dot(onehot(mine), flat, preferred_element_type=F32).astype(BF16)
        outs.append(pltpu.make_async_copy(packed.at[span], terms.at[span], sems.at[5 + i]))
        outs[-1].start()
    finish(outs)


def rotate_kernel(place, encoded, upstream, *refs):
    found, (grad, rows_in, e_in, g_in, out, sems) = refs[:-6], refs[-6:]
    size = found[0].shape[0]
    parts = [(part, rows_in.at[pl.ds(k * size, size)]) for k, part in enumerate(found)]
    copies = fetch([(encoded, e_in), (upstream, g_in)] + parts, sems)
    cells, slots = out.shape[0], rows_in.shape[0]
    column = place[...].T[:, 1:2]
    finish(copies)
    step = 256
    for i in range(cells // step):
        span = slice(i * step, (i + 1) * step)
        mine = onehot(lax.broadcasted_iota(jnp.int32, (step, slots), 1).astype(F32) == column[span])
        q = jnp.dot(mine, rows_in[...], preferred_element_type=F32)
        e = e_in[span, :].astype(F32)
        g = g_in[span, :].astype(F32)
        lat_norm = jnp.sqrt(jnp.sum(e * e, -1, keepdims=True) + 1e-06)
        quant_norm = jnp.sqrt(jnp.sum(q * q, -1, keepdims=True) + 1e-06)
        a = e / lat_norm
        b = q / quant_norm
        cosine = jnp.sum(a * b, -1, keepdims=True)
        s = a + b
        turned = g - s * (jnp.sum(s * g, -1, keepdims=True) / (1.0 + cosine))
        turned = turned + 2.0 * a * jnp.sum(b * g, -1, keepdims=True)
        out[span, :] = (quant_norm / lat_norm * turned + 2.0 * COMMIT * (e - q)).astype(BF16)
    finish(fetch([(out, grad)], sems.at[pl.ds(0, 1)]))


def sort_kernel(capacity, codes_ref, bounds_ref, order_ref, sorted_ref, named_ref):
    sources = codes_ref.shape[0]
    slots = sources * capacity
    blocks = bounds_ref.shape[0]
    chunks = slots // BLOCK
    width = codes_ref.shape[2]
    code = jnp.concatenate([codes_ref[i, 7:8, :capacity] for i in range(sources)], axis=1)
    earlier = onehot(
        lax.broadcasted_iota(jnp.int32, (width, width), 0) < lax.broadcasted_iota(jnp.int32, (width, width), 1)
    )
    block = jnp.where(code >= 0, code // BLOCK, -1)
    hits = jnp.where(lax.broadcasted_iota(jnp.int32, (blocks, slots), 0) == block, 1.0, 0.0)
    before = jnp.zeros((blocks, 1), F32)
    parts = []
    for i in range(slots // width):
        part = hits[:, i * width : (i + 1) * width]
        parts.append(jnp.dot(part.astype(BF16), earlier, preferred_element_type=F32) + before)
        before = before + jnp.sum(part, 1, keepdims=True)
    ranks = jnp.concatenate(parts, axis=1)
    counts = lax.dot_general(jnp.ones((8, slots), BF16), hits.astype(BF16), NT, preferred_element_type=F32)[0:1]
    lower = lax.broadcasted_iota(jnp.int32, (blocks, blocks), 1) < lax.broadcasted_iota(jnp.int32, (blocks, blocks), 0)
    starts = jnp.sum(jnp.where(lower, counts, 0.0), 1, keepdims=True)
    lane = lax.broadcasted_iota(jnp.int32, (blocks, width), 1)
    bounds_ref[...] = jnp.where(lane == 0, starts, starts + before).astype(jnp.int32)
    order = jnp.sum(hits * (ranks + starts), 0, keepdims=True)
    order = jnp.where(code >= 0, order, -1.0)
    order_ref[...] = order
    at = order.astype(jnp.int32)
    chunk = lax.broadcasted_iota(jnp.int32, (chunks, slots), 0) == jnp.where(at >= 0, at // BLOCK, -1)
    ones = jnp.where(chunk, 1.0, 0.0)
    picked = jnp.concatenate(
        [ones * (code // BLOCK).astype(F32), ones * (code % BLOCK).astype(F32), ones], axis=0
    ).astype(BF16)
    chosen = onehot(lax.broadcasted_iota(jnp.int32, (BLOCK, slots), 0) == at % BLOCK)
    spread = lax.dot_general(picked, chosen, NT, preferred_element_type=F32)
    inside = jnp.where(
        spread[2 * chunks :] > 0.5, spread[:chunks] * float(BLOCK) + spread[chunks : 2 * chunks], -1.0
    )
    sorted_ref[...] = jnp.full(sorted_ref.shape, -1, jnp.int32)
    sorted_ref[:chunks, :] = inside.astype(jnp.int32)
    low = onehot(lax.broadcasted_iota(jnp.int32, (BLOCK, slots), 0) == jnp.where(code >= 0, code % BLOCK, -1))
    named = lax.dot_general(low, hits.astype(BF16), NT, preferred_element_type=F32)
    named_ref[...] = jnp.zeros(named_ref.shape, F32)
    named_ref[:, :blocks] = named


def scatter_kernel(here, bounds, terms, book, order, codes, named, grad, rows_in, book_in, ranked, out, sums, sems):
    slots = rows_in.shape[0]
    chunks = slots // BLOCK
    blocks = out.shape[0] // BLOCK
    own = pl.ds(pl.multiple_of(here[0] * out.shape[0], BLOCK), out.shape[0])
    copies = fetch([(terms, rows_in), (book.at[own], book_in)], sems)
    copies[0].wait()
    at_slot = lax.broadcasted_iota(jnp.int32, (BLOCK, slots), 0).astype(F32)

    def rank(i, carry):
        mine = onehot(at_slot == order[...] - (i * BLOCK).astype(F32))
        span = pl.ds(pl.multiple_of(i * BLOCK, BLOCK), BLOCK)
        ranked[span, :] = jnp.dot(mine, rows_in[...], preferred_element_type=F32).astype(BF16)
        return carry

    lax.fori_loop(0, chunks, rank, 0)
    ranked[slots:, :] = jnp.zeros((ranked.shape[0] - slots, ranked.shape[1]), BF16)
    copies[1].wait()
    at_row = lax.broadcasted_iota(jnp.int32, (BLOCK, BLOCK), 0)
    step = 8

    def part(b, j):
        mine = onehot(at_row == codes[pl.ds(j, 1), :] - b * BLOCK)
        rows = ranked[pl.ds(pl.multiple_of(j * BLOCK, BLOCK), BLOCK), :]
        return jnp.dot(mine, rows, preferred_element_type=F32)

    def leave(b):
        span = pl.ds(pl.multiple_of(b * BLOCK, BLOCK), BLOCK)
        return pltpu.make_async_copy(out.at[span], grad.at[span], sems.at[2 + b])

    def several(g, carry):
        counts = pltpu.roll(named[...], lax.rem(named.shape[1] - g * step, named.shape[1]), 1)
        for i in range(step):
            b = g * step + i
            first = bounds[b, 0] // BLOCK
            span = pl.ds(pl.multiple_of(b * BLOCK, BLOCK), BLOCK)
            total = part(b, first) + part(b, first + 1)
            out[span, :] = (2.0 * (counts[:, i : i + 1] * book_in[span, :].astype(F32) - total)).astype(BF16)
            leave(b).start()
        return carry

    lax.fori_loop(0, blocks // step, several, 0)

    def last(b, carry):
        first = bounds[b, 0] // BLOCK
        after = (bounds[b, 1] + BLOCK - 1) // BLOCK
        leave(b).wait()

        @pl.when(after > first + 2)
        def _():
            span = pl.ds(pl.multiple_of(b * BLOCK, BLOCK), BLOCK)
            sums[...] = jnp.zeros_like(sums)

            def more(j, carry):
                sums[...] += part(b, j)
                return carry

            lax.fori_loop(first, after, more, 0)
            counts = pltpu.roll(named[...], lax.rem(named.shape[1] - b, named.shape[1]), 1)
            out[span, :] = (2.0 * (counts[:, 0:1] * book_in[span, :].astype(F32) - sums[...])).astype(BF16)
            leave(b).start()
            leave(b).wait()

        return carry

    lax.fori_loop(0, blocks, last, 0)


def shape(dims, dtype=BF16):
    return jax.ShapeDtypeStruct(tuple(dims), dtype)


def halo(video, done, asked):
    before = along(video, "tm", 1)
    frames, _, columns, channels = video.shape
    both = shape((2 * frames, 1, columns, channels))
    top, bottom = pl.pallas_call(
        join_kernel,
        out_shape=(both, both),
        in_specs=[HBM, HBM, VMEM, HBM],
        out_specs=(HBM,) * 2,
        scratch_shapes=[pltpu.VMEM((2,) + both.shape, BF16), pltpu.SemaphoreType.DMA((6,))],
        compiler_params=params(8),
    )(before, video, done, asked)
    return before, along(bottom, "height", 1), along(top, "height", -1)


def on_device(latents, conv_first, conv_second, codebook, codes, upstream):
    frames, rows, columns, channels = latents.shape
    cells = frames * rows * columns
    held = codebook.shape[0]
    tiles = lax.axis_size("tm")
    groups = lax.axis_size("height")
    owners = tiles * groups
    range_rows = held // tiles
    capacity = 2 * cells // owners
    slots = owners * capacity
    block = (frames, rows, columns, channels)
    window = pltpu.VMEM((frames + 2, rows + 2, columns, channels), BF16)
    token = shape((8, 128), F32)
    sems = pltpu.SemaphoreType.DMA
    here = jnp.stack([lax.axis_index("tm").astype(jnp.int32), lax.axis_index("height").astype(jnp.int32)])

    def alone(change, own, residual, weight, after):
        return pl.pallas_call(
            functools.partial(own_kernel, change),
            out_shape=(shape(block, F32), token),
            in_specs=[HBM, HBM, VMEM, VMEM],
            out_specs=(HBM, VMEM),
            scratch_shapes=[window, pltpu.VMEM(block, BF16), pltpu.VMEM(block, F32), sems((4,))],
            compiler_params=params(),
        )(own, residual, weight, after)

    send, place = pl.pallas_call(
        functools.partial(index_kernel, groups, tiles, held, capacity),
        out_shape=(shape((owners, 8, columns), jnp.int32), shape((8, cells), F32)),
        in_specs=[SMEM, VMEM],
        out_specs=(VMEM,) * 2,
        compiler_params=params(),
    )(here, codes.reshape(frames * rows, columns))
    asked = lax.all_to_all(send, ("tm", "height"), split_axis=0, concat_axis=0, tiled=True)
    partial, done = alone(True, latents, latents, conv_first, place)
    before, up, down = halo(latents, done, asked)
    first, active, done = pl.pallas_call(
        first_kernel,
        out_shape=(shape(block), shape(block), token),
        in_specs=[HBM] * 4 + [VMEM],
        out_specs=(HBM, HBM, VMEM),
        scratch_shapes=[
            window,
            pltpu.VMEM(block, F32),
            pltpu.VMEM(block, BF16),
            pltpu.VMEM(block, BF16),
            sems((4 + 2 * frames,)),
        ],
        compiler_params=params(),
    )(before, up, down, partial, conv_first)

    *found, done = pl.pallas_call(
        functools.partial(gather_kernel, groups),
        out_shape=(shape((slots // groups, channels)),) * groups + (token,),
        in_specs=[SMEM, HBM, HBM, VMEM],
        out_specs=(HBM,) * groups + (VMEM,),
        scratch_shapes=[
            pltpu.SMEM((groups * 8, columns), jnp.int32),
            pltpu.VMEM((groups * 8, columns), jnp.int32),
            pltpu.VMEM((slots, TILE, channels), BF16),
            pltpu.VMEM((slots, channels), BF16),
            sems((slots // BATCH,)),
            sems((groups,)),
        ],
        compiler_params=params(),
    )(here, asked.reshape(owners * 8, columns), codebook.reshape(held // TILE, TILE, channels), done)
    partial, done = alone(False, active, first, conv_second, done)
    before, up, down = halo(active, done, done)
    encoded, terms = pl.pallas_call(
        second_kernel,
        out_shape=(shape(block), shape((slots, channels))),
        in_specs=[HBM] * 4 + [VMEM] * 2,
        out_specs=(HBM,) * 2,
        scratch_shapes=[
            window,
            pltpu.VMEM(block, F32),
            pltpu.VMEM(block, BF16),
            pltpu.VMEM((slots, channels), BF16),
            sems((5 + slots // 256,)),
        ],
        compiler_params=params(),
    )(before, up, down, partial, conv_second, place)

    owner_terms = lax.all_to_all(
        terms.reshape(owners, capacity, channels), ("tm", "height"), split_axis=0, concat_axis=0, tiled=True
    )
    found = [found[0]] + [around(found[k], "height", k) for k in range(1, groups)]
    blocks = range_rows // BLOCK
    chunks = slots // BLOCK
    bounds, order, ranked, named = pl.pallas_call(
        functools.partial(sort_kernel, capacity),
        out_shape=(
            shape((blocks, 128), jnp.int32),
            shape((1, slots), F32),
            shape((-(-(chunks + 2) // 8) * 8, BLOCK), jnp.int32),
            shape((BLOCK, 128), F32),
        ),
        in_specs=[VMEM],
        out_specs=(VMEM,) * 4,
        compiler_params=params(),
    )(asked)
    grad = pl.pallas_call(
        rotate_kernel,
        out_shape=shape((cells, channels)),
        in_specs=[VMEM] + [HBM] * (2 + groups),
        out_specs=HBM,
        scratch_shapes=[pltpu.VMEM((slots, channels), BF16)] + [pltpu.VMEM((cells, channels), BF16)] * 3
        + [sems((2 + groups,))],
        compiler_params=params(),
    )(
        place,
        encoded.reshape(cells, channels),
        upstream.reshape(cells, channels),
        *found,
    )
    codebook_grad = pl.pallas_call(
        scatter_kernel,
        out_shape=shape((range_rows, channels)),
        in_specs=[SMEM, SMEM, HBM, HBM, VMEM, VMEM, VMEM],
        out_specs=HBM,
        scratch_shapes=[
            pltpu.VMEM((slots, channels), BF16),
            pltpu.VMEM((range_rows, channels), BF16),
            pltpu.VMEM((slots + 2 * BLOCK, channels), BF16),
            pltpu.VMEM((range_rows, channels), BF16),
            pltpu.VMEM((BLOCK, channels), F32),
            sems((2 + blocks,)),
        ],
        compiler_params=params(),
    )(here, bounds, owner_terms.reshape(slots, channels), codebook, order, ranked, named)
    return (grad.reshape(upstream.shape), codebook_grad)


def solution(mesh):
    return jax.shard_map(
        on_device,
        mesh=mesh,
        in_specs=(
            P("tm", "height", None, None),
            P(),
            P(),
            P("height", None),
            P("tm", "height", None),
            P("tm", "height", None, None),
        ),
        out_specs=(P("tm", "height", None, None), P(("height", "tm"), None)),
        check_vma=False,
    )
```

```python
import functools

import jax
import jax.numpy as jnp
from jax import lax
from jax.experimental import pallas as pl
from jax.experimental.pallas import tpu as pltpu
from jax.sharding import PartitionSpec as P

COMMIT = 0.25
BATCH = 64
TILE = 16
BLOCK = 256
F32 = jnp.float32
BF16 = jnp.bfloat16
VMEM = pl.BlockSpec(memory_space=pltpu.VMEM)
SMEM = pl.BlockSpec(memory_space=pltpu.SMEM)
HBM = pl.BlockSpec(memory_space=pltpu.MemorySpace.HBM)
NT = (((1,), (1,)), ((), ()))


def along(x, axis, by):
    count = lax.axis_size(axis)
    return lax.ppermute(x, axis, [(i, i + by) for i in range(count) if 0 <= i + by < count])


def around(x, axis, by):
    count = lax.axis_size(axis)
    return lax.ppermute(x, axis, [(i, (i + by) % count) for i in range(count)])


def params(megabytes=28):
    return pltpu.CompilerParams(vmem_limit_bytes=megabytes << 20)


def act(values):
    scaled = values * lax.rsqrt(jnp.mean(values * values, -1, keepdims=True) + 1e-06)
    return scaled / (1.0 + jnp.exp(-scaled))


def lanes(block):
    return jnp.concatenate([block[i : i + 1, :] for i in range(block.shape[0])], axis=1)


def fetch(pairs, sems):
    copies = [pltpu.make_async_copy(src, dst, sems.at[i]) for i, (src, dst) in enumerate(pairs)]
    for copy in copies:
        copy.start()
    return copies


def finish(copies):
    for copy in copies:
        copy.wait()


def onehot(mask):
    return jnp.where(mask, 1.0, 0.0).astype(BF16)


def index_kernel(groups, tiles, held, capacity, where_ref, codes_ref, ask_ref, low_ref, place_ref):
    lines, width = codes_ref.shape[1:]
    cells = lines * width
    owners = groups * tiles
    range_rows = held // tiles
    block_slots = tiles * capacity
    batches = block_slots // BATCH
    here = where_ref[0]
    own = lanes(codes_ref[here])
    block = own // range_rows
    target = block % tiles * groups + block // tiles
    home = own // held
    arrival = lax.rem(here - home + groups, groups)
    peers = [lanes(codes_ref[lax.rem(here + k, groups)]) for k in range(groups)]
    own_hits = lax.broadcasted_iota(jnp.int32, (owners, cells), 0) == target
    home_hits = lax.broadcasted_iota(jnp.int32, (groups, cells), 0) == arrival
    peer_hits = [peer // held == here for peer in peers]
    hits = jnp.concatenate(
        [jnp.where(own_hits, 1.0, 0.0), jnp.where(home_hits, 1.0, 0.0)] + [jnp.where(x, 1.0, 0.0) for x in peer_hits], axis=0
    )
    count = hits.shape[0]
    pad = -count % 16
    if pad:
        hits = jnp.concatenate([hits, jnp.zeros((pad, cells), F32)], axis=0)
    earlier = onehot(
        lax.broadcasted_iota(jnp.int32, (width, width), 0) < lax.broadcasted_iota(jnp.int32, (width, width), 1)
    )
    before = jnp.zeros((count + pad, 1), F32)
    parts = []
    for i in range(lines):
        part = hits[:, i * width : (i + 1) * width]
        parts.append(jnp.dot(part.astype(BF16), earlier, preferred_element_type=F32) + before)
        before = before + jnp.sum(part, 1, keepdims=True)
    ranks = jnp.concatenate(parts, axis=1)
    own_rank = jnp.sum(ranks[:owners] * hits[:owners], 0, keepdims=True)
    home_rank = jnp.sum(ranks[owners : owners + groups] * hits[owners : owners + groups], 0, keepdims=True)
    place_ref[0:1, :] = target.astype(F32) * capacity + own_rank
    place_ref[1:2, :] = arrival.astype(F32) * block_slots + home_rank
    place_ref[2:, :] = jnp.zeros((6, cells), F32)
    columns = []
    for k in range(groups):
        hit = hits[owners + groups + k : owners + groups + k + 1]
        rank = ranks[owners + groups + k : owners + groups + k + 1].astype(jnp.int32)
        row = jnp.where(peer_hits[k], peers[k] - here * held, 0)
        batch = onehot(
            lax.broadcasted_iota(jnp.int32, (batches, cells), 0) == jnp.where(peer_hits[k], rank // BATCH, -1)
        ).astype(F32)
        tile = row // TILE
        picked = jnp.concatenate(
            [
                batch * (tile // 128).astype(F32),
                batch * (tile % 128).astype(F32),
                batch,
                batch * (row % TILE).astype(F32),
            ],
            axis=0,
        ).astype(BF16)
        chosen = onehot(lax.broadcasted_iota(jnp.int32, (BATCH, cells), 0) == rank % BATCH)
        slots = lax.dot_general(picked, chosen, NT, preferred_element_type=F32)
        asked = slots[:batches] * 128.0 + slots[batches : 2 * batches]
        ask_ref[k * batches : (k + 1) * batches, :] = jnp.where(
            slots[2 * batches : 3 * batches] > 0.5, asked, -1.0
        ).astype(jnp.int32)
        columns.append(lax.dot_general(chosen, picked[3 * batches :], NT, preferred_element_type=F32))
    low_ref[...] = jnp.concatenate(columns, axis=1)


def gather_kernel(which, ask_ref, book_ref, low_ref, _, *refs):
    groups = len(which)
    outs, (done, land, out, sems, out_sems) = refs[:groups], refs[groups:]
    done[...] = jnp.zeros_like(done)
    total = out.shape[0] // BATCH
    skip = which[0] * (total // groups)

    def copy_in(g):
        def one(i, carry):
            tile = jnp.maximum(ask_ref[skip + g, i], 0)
            pltpu.make_async_copy(book_ref.at[tile], land.at[g * BATCH + i], sems.at[g]).start()
            return carry

        lax.fori_loop(0, BATCH, one, 0, unroll=16)

    for g in range(total):
        pl.when(ask_ref[skip + g, 0] >= 0)(functools.partial(copy_in, g))
    at = lax.broadcasted_iota(jnp.int32, (BATCH, BATCH * TILE), 1)
    at = at - TILE * lax.broadcasted_iota(jnp.int32, (BATCH, BATCH * TILE), 0)
    at = at.astype(F32)
    for g in range(total):
        span = slice(g * BATCH, (g + 1) * BATCH)
        filled = ask_ref[skip + g, 0] >= 0

        @pl.when(filled)
        def _(g=g, span=span):
            block = land.at[pl.ds(g * BATCH, BATCH)]
            pltpu.make_async_copy(book_ref.at[pl.ds(0, BATCH)], block, sems.at[g]).wait()
            tiles = land[span].reshape(BATCH * TILE, land.shape[-1])
            out[span, :] = jnp.dot(onehot(at == low_ref[:, skip + g : skip + g + 1]), tiles, preferred_element_type=F32).astype(BF16)

        @pl.when(jnp.logical_not(filled))
        def _(span=span):
            out[span, :] = jnp.zeros((BATCH, out.shape[-1]), BF16)

    size = out.shape[0] // groups
    finish(fetch([(out.at[pl.ds(k * size, size)], outs[k]) for k in range(groups)], out_sems))


def double(own, other, both):
    count = own.shape[0]
    both[:count] = own[...]
    both[count:] = other[...]


def join_kernel(before, own, _, codes, others, top, bottom, codes_out, done, held, sems):
    done[...] = jnp.zeros_like(done)
    double(codes, others, codes_out)
    frames, rows = own.shape[:2]
    old, new = pl.ds(0, frames), pl.ds(frames, frames)
    first, last = pl.ds(0, 1), pl.ds(rows - 1, 1)
    ins = fetch(
        [
            (before.at[:, first], held.at[0, old]),
            (own.at[:, first], held.at[0, new]),
            (before.at[:, last], held.at[1, old]),
            (own.at[:, last], held.at[1, new]),
        ],
        sems,
    )
    finish(ins[2:])
    outs = fetch([(held.at[1], bottom)], sems.at[pl.ds(4, 1)])
    finish(ins[:2])
    outs += fetch([(held.at[0], top)], sems.at[pl.ds(5, 1)])
    finish(outs)


def taps(patch, weight, columns):
    flat = patch.shape[0]
    place = lax.broadcasted_iota(jnp.int32, (flat, 1), 0) % columns
    sums = [jnp.dot(patch, weight(r), preferred_element_type=F32) for r in range(3)]
    left = jnp.where(place == 0, 0.0, pltpu.roll(sums[0], 1, 0))
    right = jnp.where(place == columns - 1, 0.0, pltpu.roll(sums[2], flat - 1, 0))
    return sums[1] + left + right


def frame_taps(window, weight, frame, count):
    rows, columns, channels = window.shape[1] - 2, window.shape[2], window.shape[3]
    pieces = [
        window[frame : frame + count, q : q + rows].reshape(count * rows * columns, channels) for q in range(3)
    ]
    return taps(jnp.concatenate(pieces, axis=1), weight, columns).reshape(count, rows, columns, channels)


def edge_taps(window, weight, side):
    columns, channels = window.shape[2], window.shape[3]
    row, q = (0, 0) if side == 0 else (window.shape[1] - 1, 2)
    one, two = window[2, row], window[3, row]
    before = jnp.concatenate([jnp.zeros_like(one), one], axis=0)
    patch = jnp.concatenate([before, jnp.concatenate([one, two], axis=0)], axis=1)
    return taps(
        patch, lambda r: weight[1:, q, r].reshape(2 * channels, channels), columns
    ).reshape(2, 1, columns, channels)


def own_kernel(change, own, residual, weight, *refs):
    partial, done, window, source, taken, result, sems = refs[-7:]
    frames, rows, columns, channels = source.shape
    copies = fetch(
        [
            (own, window.at[pl.ds(2, frames), pl.ds(1, rows)]),
            (weight.at[2], taken.at[1]),
            (residual, source),
            (weight.at[1], taken.at[0]),
        ],
        sems,
    )
    empty = jnp.zeros((frames, 1, columns, channels), BF16)
    window[2:, 0:1] = empty
    window[2:, rows + 1 :] = empty
    done[...] = jnp.zeros_like(done)
    copies[0].wait()
    if change:
        for f in range(2, frames + 2):
            window[f, 1 : rows + 1] = act(window[f, 1 : rows + 1].astype(F32)).astype(BF16)
    finish(copies[1:3])
    wide = 3 * channels
    result[...] = source[...].astype(F32) + frame_taps(
        window, lambda r: taken[1, :, r].reshape(wide, channels), 2, 2
    )
    first = fetch([(result.at[0], partial.at[0])], sems.at[pl.ds(4, 1)])
    copies[3].wait()
    result[1] += frame_taps(window, lambda r: taken[0, :, r].reshape(wide, channels), 2, 1)[0]
    finish(first + fetch([(result.at[1], partial.at[1])], sems.at[pl.ds(5, 1)]))


def own_second_kernel(own, residual, weight, _, partial, window, source, result, sems):
    frames, rows, columns, channels = source.shape
    copies = fetch([(own, window.at[pl.ds(2, frames), pl.ds(1, rows)]), (residual, source)], sems)
    empty = jnp.zeros((frames, 1, columns, channels), BF16)
    window[2:, 0:1] = empty
    window[2:, rows + 1 :] = empty
    finish(copies)
    wide = 3 * channels
    result[...] = source[...].astype(F32) + frame_taps(
        window, lambda r: weight[2, :, r].reshape(wide, channels), 2, 2
    )
    first = fetch([(result.at[0], partial.at[0])], sems.at[pl.ds(2, 1)])
    result[1] += frame_taps(window, lambda r: weight[1, :, r].reshape(wide, channels), 2, 1)[0]
    finish(first + fetch([(result.at[1], partial.at[1])], sems.at[pl.ds(3, 1)]))


def rest(change, before, up, down, partial, weight, window, total, sems):
    frames, rows, columns, channels = total.shape
    copies = fetch(
        [
            (before, window.at[pl.ds(0, 2), pl.ds(1, rows)]),
            (up, window.at[:, pl.ds(0, 1)]),
            (down, window.at[:, pl.ds(rows + 1, 1)]),
            (partial, total),
        ],
        sems,
    )
    finish(copies[:3])
    if change:
        for f in range(frames + 2):
            for span in (slice(0, rows + 2),) if f < 2 else (slice(0, 1), slice(rows + 1, rows + 2)):
                window[f, span] = act(window[f, span].astype(F32)).astype(BF16)
    copies[3].wait()
    wide = 3 * channels
    total[...] += frame_taps(window, lambda r: weight[0, :, r].reshape(wide, channels), 0, 2)
    total[0:1] += frame_taps(window, lambda r: weight[1, :, r].reshape(wide, channels), 1, 1)
    total[:, 0:1] += edge_taps(window, weight, 0)
    total[:, -1:] += edge_taps(window, weight, 1)


def first_kernel(
    before, up, down, partial, weight, codes, others, first, active, codes_out, done, window, total, a, b, sems
):
    done[...] = jnp.zeros_like(done)
    double(codes, others, codes_out)
    rest(True, before, up, down, partial, weight, window, total, sems)
    outs = []
    for f in range(total.shape[0]):
        a[f] = total[f].astype(BF16)
        b[f] = act(a[f].astype(F32)).astype(BF16)
        for i, (src, dst) in enumerate(((b, active), (a, first))):
            outs.append(pltpu.make_async_copy(src.at[f], dst.at[f], sems.at[4 + 2 * f + i]))
            outs[-1].start()
    finish(outs)


def second_kernel(before, up, down, partial, weight, place, codes, others, *refs):
    encoded, terms, codes_out, done, window, total, a, packed, sems = refs
    done[...] = jnp.zeros_like(done)
    double(codes, others, codes_out)
    rest(False, before, up, down, partial, weight, window, total, sems)
    frames, rows, columns, channels = total.shape
    a[...] = total[...].astype(BF16)
    outs = fetch([(a, encoded)], sems.at[pl.ds(4, 1)])
    flat = a[...].reshape(frames * rows * columns, channels)
    cells = flat.shape[0]
    step = 256
    for i in range(packed.shape[0] // step):
        mine = lax.broadcasted_iota(jnp.int32, (step, cells), 0).astype(F32) + float(i * step) == place[0:1, :]
        span = pl.ds(i * step, step)
        packed[span, :] = jnp.dot(onehot(mine), flat, preferred_element_type=F32).astype(BF16)
        outs.append(pltpu.make_async_copy(packed.at[span], terms.at[span], sems.at[5 + i]))
        outs[-1].start()
    finish(outs)


def rotate_kernel(place, encoded, upstream, *refs):
    found, (grad, rows_in, e_in, g_in, out, sems) = refs[:-6], refs[-6:]
    size = found[0].shape[0]
    parts = [(part, rows_in.at[pl.ds(k * size, size)]) for k, part in enumerate(found)]
    copies = fetch([(encoded, e_in), (upstream, g_in)] + parts, sems)
    cells, slots = out.shape[0], rows_in.shape[0]
    column = place[...].T[:, 1:2]
    finish(copies)
    step = 256
    for i in range(cells // step):
        span = slice(i * step, (i + 1) * step)
        mine = onehot(lax.broadcasted_iota(jnp.int32, (step, slots), 1).astype(F32) == column[span])
        q = jnp.dot(mine, rows_in[...], preferred_element_type=F32)
        e = e_in[span, :].astype(F32)
        g = g_in[span, :].astype(F32)
        lat_norm = jnp.sqrt(jnp.sum(e * e, -1, keepdims=True) + 1e-06)
        quant_norm = jnp.sqrt(jnp.sum(q * q, -1, keepdims=True) + 1e-06)
        a = e / lat_norm
        b = q / quant_norm
        cosine = jnp.sum(a * b, -1, keepdims=True)
        s = a + b
        turned = g - s * (jnp.sum(s * g, -1, keepdims=True) / (1.0 + cosine))
        turned = turned + 2.0 * a * jnp.sum(b * g, -1, keepdims=True)
        out[span, :] = (quant_norm / lat_norm * turned + 2.0 * COMMIT * (e - q)).astype(BF16)
    finish(fetch([(out, grad)], sems.at[pl.ds(0, 1)]))


def sort_kernel(tiles, capacity, near, here, every, bounds_ref, order_ref, sorted_ref, named_ref, codes_ref):
    groups = every.shape[0] // tiles
    for k in range(tiles):
        codes_ref[pl.ds((near[0] ^ k) * groups, groups)] = every[k * groups : (k + 1) * groups]
    sources, lines, width = codes_ref.shape
    rows = bounds_ref.shape[0] * BLOCK
    mine = (here[0] * tiles + near[0]) * rows
    cells = lines * width
    slots = sources * capacity
    blocks = bounds_ref.shape[0]
    chunks = slots // BLOCK
    earlier = onehot(
        lax.broadcasted_iota(jnp.int32, (width, width), 0) < lax.broadcasted_iota(jnp.int32, (width, width), 1)
    )
    parts, ranks = [], []
    before = jnp.zeros((sources, 1), F32)
    for i in range(lines):
        local = codes_ref[:, i, :] - mine
        inside = (local >= 0) & (local < rows)
        part = jnp.where(inside, 1.0, 0.0)
        rank = jnp.dot(part.astype(BF16), earlier, preferred_element_type=F32) + before
        before = before + jnp.sum(part, 1, keepdims=True)
        parts.append(jnp.where(inside, local, -1))
        ranks.append(jnp.where(inside, rank, -1.0))
    parts, ranks = jnp.concatenate(parts, axis=1), jnp.concatenate(ranks, axis=1)
    picked_high = jnp.where(parts >= 0, parts // 256, 0).astype(F32)
    picked_low = jnp.where(parts >= 0, parts % 256, 0).astype(F32)
    picked_one = jnp.where(parts >= 0, 1.0, 0.0)
    slot = lax.broadcasted_iota(jnp.int32, (capacity, cells), 0).astype(F32)
    found = []
    for i in range(sources):
        span = slice(i, i + 1)
        picked = jnp.concatenate(
            [picked_high[span], picked_low[span], picked_one[span], jnp.zeros((5, cells), F32)], axis=0
        )
        found.append(
            lax.dot_general(picked.astype(BF16), onehot(slot == ranks[span]), NT, preferred_element_type=F32)
        )
    found = jnp.concatenate(found, axis=1)
    code = jnp.where(found[2:3] > 0.5, found[0:1] * 256.0 + found[1:2], -1.0).astype(jnp.int32)
    block = jnp.where(code >= 0, code // BLOCK, -1)
    hits = jnp.where(lax.broadcasted_iota(jnp.int32, (blocks, slots), 0) == block, 1.0, 0.0)
    before = jnp.zeros((blocks, 1), F32)
    parts = []
    for i in range(slots // width):
        part = hits[:, i * width : (i + 1) * width]
        parts.append(jnp.dot(part.astype(BF16), earlier, preferred_element_type=F32) + before)
        before = before + jnp.sum(part, 1, keepdims=True)
    ranks = jnp.concatenate(parts, axis=1)
    counts = lax.dot_general(jnp.ones((8, slots), BF16), hits.astype(BF16), NT, preferred_element_type=F32)[0:1]
    lower = lax.broadcasted_iota(jnp.int32, (blocks, blocks), 1) < lax.broadcasted_iota(jnp.int32, (blocks, blocks), 0)
    starts = jnp.sum(jnp.where(lower, counts, 0.0), 1, keepdims=True)
    lane = lax.broadcasted_iota(jnp.int32, (blocks, width), 1)
    bounds_ref[...] = jnp.where(lane == 0, starts, starts + before).astype(jnp.int32)
    order = jnp.sum(hits * (ranks + starts), 0, keepdims=True)
    order = jnp.where(code >= 0, order, -1.0)
    order_ref[...] = order
    at = order.astype(jnp.int32)
    chunk = lax.broadcasted_iota(jnp.int32, (chunks, slots), 0) == jnp.where(at >= 0, at // BLOCK, -1)
    ones = jnp.where(chunk, 1.0, 0.0)
    picked = jnp.concatenate(
        [ones * (code // BLOCK).astype(F32), ones * (code % BLOCK).astype(F32), ones], axis=0
    ).astype(BF16)
    chosen = onehot(lax.broadcasted_iota(jnp.int32, (BLOCK, slots), 0) == at % BLOCK)
    spread = lax.dot_general(picked, chosen, NT, preferred_element_type=F32)
    inside = jnp.where(
        spread[2 * chunks :] > 0.5, spread[:chunks] * float(BLOCK) + spread[chunks : 2 * chunks], -1.0
    )
    sorted_ref[...] = jnp.full(sorted_ref.shape, -1, jnp.int32)
    sorted_ref[:chunks, :] = inside.astype(jnp.int32)
    low = onehot(lax.broadcasted_iota(jnp.int32, (BLOCK, slots), 0) == jnp.where(code >= 0, code % BLOCK, -1))
    named = lax.dot_general(low, hits.astype(BF16), NT, preferred_element_type=F32)
    named_ref[...] = jnp.zeros(named_ref.shape, F32)
    named_ref[:, :blocks] = named


def scatter_kernel(here, bounds, terms, book, order, codes, named, grad, rows_in, book_in, ranked, out, sums, sems):
    slots = rows_in.shape[0]
    chunks = slots // BLOCK
    blocks = out.shape[0] // BLOCK
    own = pl.ds(pl.multiple_of(here[0] * out.shape[0], BLOCK), out.shape[0])
    copies = fetch([(terms, rows_in), (book.at[own], book_in)], sems)
    copies[0].wait()
    at_slot = lax.broadcasted_iota(jnp.int32, (BLOCK, slots), 0).astype(F32)

    def rank(i, carry):
        mine = onehot(at_slot == order[...] - (i * BLOCK).astype(F32))
        span = pl.ds(pl.multiple_of(i * BLOCK, BLOCK), BLOCK)
        ranked[span, :] = jnp.dot(mine, rows_in[...], preferred_element_type=F32).astype(BF16)
        return carry

    lax.fori_loop(0, chunks, rank, 0)
    ranked[slots:, :] = jnp.zeros((ranked.shape[0] - slots, ranked.shape[1]), BF16)
    copies[1].wait()
    at_row = lax.broadcasted_iota(jnp.int32, (BLOCK, BLOCK), 0)
    step = 8

    def part(b, j):
        mine = onehot(at_row == codes[pl.ds(j, 1), :] - b * BLOCK)
        rows = ranked[pl.ds(pl.multiple_of(j * BLOCK, BLOCK), BLOCK), :]
        return jnp.dot(mine, rows, preferred_element_type=F32)

    def leave(b):
        span = pl.ds(pl.multiple_of(b * BLOCK, BLOCK), BLOCK)
        return pltpu.make_async_copy(out.at[span], grad.at[span], sems.at[2 + b])

    def several(g, carry):
        counts = pltpu.roll(named[...], lax.rem(named.shape[1] - g * step, named.shape[1]), 1)
        for i in range(step):
            b = g * step + i
            first = bounds[b, 0] // BLOCK
            span = pl.ds(pl.multiple_of(b * BLOCK, BLOCK), BLOCK)
            total = part(b, first) + part(b, first + 1)
            out[span, :] = (2.0 * (counts[:, i : i + 1] * book_in[span, :].astype(F32) - total)).astype(BF16)
            leave(b).start()
        return carry

    lax.fori_loop(0, blocks // step, several, 0)

    def last(b, carry):
        first = bounds[b, 0] // BLOCK
        after = (bounds[b, 1] + BLOCK - 1) // BLOCK
        leave(b).wait()

        @pl.when(after > first + 2)
        def _():
            span = pl.ds(pl.multiple_of(b * BLOCK, BLOCK), BLOCK)
            sums[...] = jnp.zeros_like(sums)

            def more(j, carry):
                sums[...] += part(b, j)
                return carry

            lax.fori_loop(first, after, more, 0)
            counts = pltpu.roll(named[...], lax.rem(named.shape[1] - b, named.shape[1]), 1)
            out[span, :] = (2.0 * (counts[:, 0:1] * book_in[span, :].astype(F32) - sums[...])).astype(BF16)
            leave(b).start()
            leave(b).wait()

        return carry

    lax.fori_loop(0, blocks, last, 0)


def shape(dims, dtype=BF16):
    return jax.ShapeDtypeStruct(tuple(dims), dtype)


def halo(video, after, codes, others):
    before = along(video, "tm", 1)
    frames, _, columns, channels = video.shape
    both = shape((2 * frames, 1, columns, channels))
    more = shape((2 * codes.shape[0],) + codes.shape[1:], jnp.int32)
    top, bottom, codes, done = pl.pallas_call(
        join_kernel,
        out_shape=(both, both, more, shape((8, 128), F32)),
        in_specs=[HBM] * 2 + [VMEM] * 3,
        out_specs=(HBM, HBM, VMEM, VMEM),
        scratch_shapes=[pltpu.VMEM((2,) + both.shape, BF16), pltpu.SemaphoreType.DMA((6,))],
        compiler_params=params(),
    )(before, video, after, codes, others)
    return before, along(bottom, "height", 1), along(top, "height", -1), codes, done


def swapped(codes, axis, by):
    count = lax.axis_size(axis)
    return lax.ppermute(codes, axis, [(i, i ^ by) for i in range(count)])


def on_device(latents, conv_first, conv_second, codebook, codes, upstream):
    frames, rows, columns, channels = latents.shape
    cells = frames * rows * columns
    held = codebook.shape[0]
    tiles = lax.axis_size("tm")
    groups = lax.axis_size("height")
    owners = tiles * groups
    range_rows = held // tiles
    capacity = 2 * cells // owners
    slots = owners * capacity
    block = (frames, rows, columns, channels)
    window = pltpu.VMEM((frames + 2, rows + 2, columns, channels), BF16)
    whole = pltpu.VMEM(block, F32)
    half = pltpu.VMEM(block, BF16)
    token = shape((8, 128), F32)
    sems = pltpu.SemaphoreType.DMA
    near = lax.axis_index("tm").astype(jnp.int32).reshape(1)
    here = lax.axis_index("height").astype(jnp.int32).reshape(1)

    def code_lines(count):
        return shape((count * groups, frames * rows, columns), jnp.int32)

    shared = lax.all_gather(codes.reshape(frames * rows, columns), "height")
    ask, low, place = pl.pallas_call(
        functools.partial(index_kernel, groups, tiles, held, capacity),
        out_shape=(
            shape((slots // BATCH, BATCH), jnp.int32),
            shape((BATCH, slots // BATCH), F32),
            shape((8, cells), F32),
        ),
        in_specs=[SMEM, VMEM],
        out_specs=(VMEM,) * 3,
        compiler_params=params(),
    )(here, shared)
    every = shared
    by = 1
    while by * 8 < tiles:
        every = jnp.concatenate([every, swapped(every, "tm", by)])
        by *= 2
    partial, done = pl.pallas_call(
        functools.partial(own_kernel, True),
        out_shape=(shape(block, F32), token),
        in_specs=[HBM] * 4,
        out_specs=(HBM, VMEM),
        scratch_shapes=[window, half, pltpu.VMEM((2, 3, 3, channels, channels), BF16), whole, sems((6,))],
        compiler_params=params(28),
    )(latents, latents, conv_first, place)
    before, up, down, _, done = halo(latents, done, shared, shared)
    first, active, every, done = pl.pallas_call(
        first_kernel,
        out_shape=(shape(block), shape(block), code_lines(2 * by), token),
        in_specs=[HBM] * 4 + [VMEM] * 3,
        out_specs=(HBM, HBM, VMEM, VMEM),
        scratch_shapes=[window, whole, half, half, sems((4 + 2 * frames,))],
        compiler_params=params(),
    )(before, up, down, partial, conv_first, every, swapped(every, "tm", by))
    by *= 2

    def lookup(which, after):
        return pl.pallas_call(
            functools.partial(gather_kernel, which),
            out_shape=(shape((slots // groups, channels)),) * len(which) + (token,),
            in_specs=[SMEM, HBM, VMEM, VMEM],
            out_specs=(HBM,) * len(which) + (VMEM,),
            scratch_shapes=[
                pltpu.VMEM((slots // groups * len(which), TILE, channels), BF16),
                pltpu.VMEM((slots // groups * len(which), channels), BF16),
                sems((slots // groups * len(which) // BATCH,)),
                sems((len(which),)),
            ],
            compiler_params=params(),
        )(ask, codebook.reshape(held // TILE, TILE, channels), low, after)

    *found, done = lookup(range(1, groups), done)
    before, up, down, every, done = halo(active, done, every, swapped(every, "tm", by))
    by *= 2
    partial = pl.pallas_call(
        own_second_kernel,
        out_shape=shape(block, F32),
        in_specs=[HBM] * 2 + [VMEM] * 2,
        out_specs=HBM,
        scratch_shapes=[window, half, whole, sems((4,))],
        compiler_params=params(),
    )(active, first, conv_second, done)
    encoded, terms, every, done = pl.pallas_call(
        second_kernel,
        out_shape=(shape(block), shape((slots, channels)), code_lines(2 * by), token),
        in_specs=[HBM] * 4 + [VMEM] * 4,
        out_specs=(HBM, HBM, VMEM, VMEM),
        scratch_shapes=[window, whole, half, pltpu.VMEM((slots, channels), BF16), sems((5 + slots // 256,))],
        compiler_params=params(),
    )(before, up, down, partial, conv_second, place, every, swapped(every, "tm", by))

    owner_terms = lax.all_to_all(
        terms.reshape(owners, capacity, channels), ("tm", "height"), split_axis=0, concat_axis=0, tiled=True
    )
    found = [around(rows_of, "height", k + 1) for k, rows_of in enumerate(found)]
    found = [lookup(range(1), done)[0]] + found
    blocks = range_rows // BLOCK
    chunks = slots // BLOCK
    bounds, order, ranked, named = pl.pallas_call(
        functools.partial(sort_kernel, tiles, capacity),
        out_shape=(
            shape((blocks, 128), jnp.int32),
            shape((1, slots), F32),
            shape((-(-(chunks + 2) // 8) * 8, BLOCK), jnp.int32),
            shape((BLOCK, 128), F32),
        ),
        in_specs=[SMEM, SMEM, VMEM],
        out_specs=(VMEM,) * 4,
        scratch_shapes=[pltpu.VMEM((owners, frames * rows, columns), jnp.int32)],
        compiler_params=params(),
    )(near, here, every)
    grad = pl.pallas_call(
        rotate_kernel,
        out_shape=shape((cells, channels)),
        in_specs=[VMEM] + [HBM] * (2 + groups),
        out_specs=HBM,
        scratch_shapes=[pltpu.VMEM((slots, channels), BF16)] + [pltpu.VMEM((cells, channels), BF16)] * 3
        + [sems((2 + groups,))],
        compiler_params=params(),
    )(
        place,
        encoded.reshape(cells, channels),
        upstream.reshape(cells, channels),
        *found,
    )
    codebook_grad = pl.pallas_call(
        scatter_kernel,
        out_shape=shape((range_rows, channels)),
        in_specs=[SMEM, SMEM, HBM, HBM, VMEM, VMEM, VMEM],
        out_specs=HBM,
        scratch_shapes=[
            pltpu.VMEM((slots, channels), BF16),
            pltpu.VMEM((range_rows, channels), BF16),
            pltpu.VMEM((slots + 2 * BLOCK, channels), BF16),
            pltpu.VMEM((range_rows, channels), BF16),
            pltpu.VMEM((BLOCK, channels), F32),
            sems((2 + blocks,)),
        ],
        compiler_params=params(),
    )(near, bounds, owner_terms.reshape(slots, channels), codebook, order, ranked, named)
    return (grad.reshape(upstream.shape), codebook_grad)


def solution(mesh):
    return jax.shard_map(
        on_device,
        mesh=mesh,
        in_specs=(
            P("tm", "height", None, None),
            P(),
            P(),
            P("height", None),
            P("tm", "height", None),
            P("tm", "height", None, None),
        ),
        out_specs=(P("tm", "height", None, None), P(("height", "tm"), None)),
        check_vma=False,
    )
```

```python
import functools

import jax
import jax.numpy as jnp
from jax import lax
from jax.experimental import pallas as pl
from jax.experimental.pallas import tpu as pltpu
from jax.sharding import PartitionSpec as P

COMMIT = 0.25
BATCH = 64
TILE = 16
BLOCK = 256
F32 = jnp.float32
BF16 = jnp.bfloat16
VMEM = pl.BlockSpec(memory_space=pltpu.VMEM)
SMEM = pl.BlockSpec(memory_space=pltpu.SMEM)
HBM = pl.BlockSpec(memory_space=pltpu.MemorySpace.HBM)
NT = (((1,), (1,)), ((), ()))


def along(x, axis, by):
    count = lax.axis_size(axis)
    return lax.ppermute(x, axis, [(i, i + by) for i in range(count) if 0 <= i + by < count])


def around(x, axis, by):
    count = lax.axis_size(axis)
    return lax.ppermute(x, axis, [(i, (i + by) % count) for i in range(count)])


def params(megabytes=28):
    return pltpu.CompilerParams(vmem_limit_bytes=megabytes << 20)


def act(values):
    scaled = values * lax.rsqrt(jnp.mean(values * values, -1, keepdims=True) + 1e-06)
    return scaled / (1.0 + jnp.exp(-scaled))


def lanes(block):
    return jnp.concatenate([block[i : i + 1, :] for i in range(block.shape[0])], axis=1)


def fetch(pairs, sems):
    copies = [pltpu.make_async_copy(src, dst, sems.at[i]) for i, (src, dst) in enumerate(pairs)]
    for copy in copies:
        copy.start()
    return copies


def finish(copies):
    for copy in copies:
        copy.wait()


def rows16(width):
    return lax.broadcasted_iota(jnp.int32, (BLOCK, width), 0).astype(jnp.int16)


def onehot16(mask):
    return jnp.where(mask, jnp.bfloat16(1), jnp.bfloat16(0))


def onehot(mask):
    return jnp.where(mask, 1.0, 0.0).astype(BF16)


def index_kernel(groups, tiles, held, capacity, where_ref, codes_ref, ask_ref, low_ref, place_ref):
    lines, width = codes_ref.shape[1:]
    cells = lines * width
    owners = groups * tiles
    range_rows = held // tiles
    block_slots = tiles * capacity
    batches = block_slots // BATCH
    here = where_ref[0]
    own = lanes(codes_ref[here])
    block = own // range_rows
    target = block % tiles * groups + block // tiles
    home = own // held
    arrival = lax.rem(here - home + groups, groups)
    peers = [lanes(codes_ref[lax.rem(here + k, groups)]) for k in range(groups)]
    own_hits = lax.broadcasted_iota(jnp.int32, (owners, cells), 0) == target
    home_hits = lax.broadcasted_iota(jnp.int32, (groups, cells), 0) == arrival
    peer_hits = [peer // held == here for peer in peers]
    hits = jnp.concatenate(
        [jnp.where(own_hits, 1.0, 0.0), jnp.where(home_hits, 1.0, 0.0)] + [jnp.where(x, 1.0, 0.0) for x in peer_hits], axis=0
    )
    count = hits.shape[0]
    pad = -count % 16
    if pad:
        hits = jnp.concatenate([hits, jnp.zeros((pad, cells), F32)], axis=0)
    earlier = onehot(
        lax.broadcasted_iota(jnp.int32, (width, width), 0) < lax.broadcasted_iota(jnp.int32, (width, width), 1)
    )
    before = jnp.zeros((count + pad, 1), F32)
    parts = []
    for i in range(lines):
        part = hits[:, i * width : (i + 1) * width]
        parts.append(jnp.dot(part.astype(BF16), earlier, preferred_element_type=F32) + before)
        before = before + jnp.sum(part, 1, keepdims=True)
    ranks = jnp.concatenate(parts, axis=1)
    own_rank = jnp.sum(ranks[:owners] * hits[:owners], 0, keepdims=True)
    home_rank = jnp.sum(ranks[owners : owners + groups] * hits[owners : owners + groups], 0, keepdims=True)
    place_ref[0:1, :] = target.astype(F32) * capacity + own_rank
    place_ref[1:2, :] = arrival.astype(F32) * block_slots + home_rank
    place_ref[2:, :] = jnp.zeros((6, cells), F32)
    columns = []
    for k in range(groups):
        hit = hits[owners + groups + k : owners + groups + k + 1]
        rank = ranks[owners + groups + k : owners + groups + k + 1].astype(jnp.int32)
        row = jnp.where(peer_hits[k], peers[k] - here * held, 0)
        batch = onehot(
            lax.broadcasted_iota(jnp.int32, (batches, cells), 0) == jnp.where(peer_hits[k], rank // BATCH, -1)
        ).astype(F32)
        tile = row // TILE
        picked = jnp.concatenate(
            [
                batch * (tile // 128).astype(F32),
                batch * (tile % 128).astype(F32),
                batch,
                batch * (row % TILE).astype(F32),
            ],
            axis=0,
        ).astype(BF16)
        chosen = onehot(lax.broadcasted_iota(jnp.int32, (BATCH, cells), 0) == rank % BATCH)
        slots = lax.dot_general(picked, chosen, NT, preferred_element_type=F32)
        asked = slots[:batches] * 128.0 + slots[batches : 2 * batches]
        ask_ref[k * batches : (k + 1) * batches, :] = jnp.where(
            slots[2 * batches : 3 * batches] > 0.5, asked, -1.0
        ).astype(jnp.int32)
        columns.append(lax.dot_general(chosen, picked[3 * batches :], NT, preferred_element_type=F32))
    low_ref[...] = jnp.concatenate(columns, axis=1)


def gather_kernel(which, ask_ref, book_ref, low_ref, _, *refs):
    groups = len(which)
    outs, (done, land, out, sems, out_sems) = refs[:groups], refs[groups:]
    done[...] = jnp.zeros_like(done)
    total = out.shape[0] // BATCH
    skip = which[0] * (total // groups)

    def copy_in(g):
        def one(i, carry):
            tile = jnp.maximum(ask_ref[skip + g, i], 0)
            pltpu.make_async_copy(book_ref.at[tile], land.at[g * BATCH + i], sems.at[g]).start()
            return carry

        lax.fori_loop(0, BATCH, one, 0, unroll=16)

    for g in range(total):
        pl.when(ask_ref[skip + g, 0] >= 0)(functools.partial(copy_in, g))
    at = lax.broadcasted_iota(jnp.int32, (BATCH, BATCH * TILE), 1)
    at = at - TILE * lax.broadcasted_iota(jnp.int32, (BATCH, BATCH * TILE), 0)
    at = at.astype(F32)
    for g in range(total):
        span = slice(g * BATCH, (g + 1) * BATCH)
        filled = ask_ref[skip + g, 0] >= 0

        @pl.when(filled)
        def _(g=g, span=span):
            block = land.at[pl.ds(g * BATCH, BATCH)]
            pltpu.make_async_copy(book_ref.at[pl.ds(0, BATCH)], block, sems.at[g]).wait()
            tiles = land[span].reshape(BATCH * TILE, land.shape[-1])
            out[span, :] = jnp.dot(onehot(at == low_ref[:, skip + g : skip + g + 1]), tiles, preferred_element_type=F32).astype(BF16)

        @pl.when(jnp.logical_not(filled))
        def _(span=span):
            out[span, :] = jnp.zeros((BATCH, out.shape[-1]), BF16)

    size = out.shape[0] // groups
    finish(fetch([(out.at[pl.ds(k * size, size)], outs[k]) for k in range(groups)], out_sems))


def double(own, other, both):
    count = own.shape[0]
    both[:count] = own[...]
    both[count:] = other[...]


def join_kernel(before, own, _, codes, others, top, bottom, codes_out, done, held, sems):
    done[...] = jnp.zeros_like(done)
    double(codes, others, codes_out)
    frames, rows = own.shape[:2]
    old, new = pl.ds(0, frames), pl.ds(frames, frames)
    first, last = pl.ds(0, 1), pl.ds(rows - 1, 1)
    ins = fetch(
        [
            (before.at[:, first], held.at[0, old]),
            (own.at[:, first], held.at[0, new]),
            (before.at[:, last], held.at[1, old]),
            (own.at[:, last], held.at[1, new]),
        ],
        sems,
    )
    finish(ins[2:])
    outs = fetch([(held.at[1], bottom)], sems.at[pl.ds(4, 1)])
    finish(ins[:2])
    outs += fetch([(held.at[0], top)], sems.at[pl.ds(5, 1)])
    finish(outs)


def taps(patch, weight, columns):
    flat = patch.shape[0]
    place = lax.broadcasted_iota(jnp.int32, (flat, 1), 0) % columns
    sums = [jnp.dot(patch, weight(r), preferred_element_type=F32) for r in range(3)]
    left = jnp.where(place == 0, 0.0, pltpu.roll(sums[0], 1, 0))
    right = jnp.where(place == columns - 1, 0.0, pltpu.roll(sums[2], flat - 1, 0))
    return sums[1] + left + right


def frame_taps(window, weight, frame, count):
    rows, columns, channels = window.shape[1] - 2, window.shape[2], window.shape[3]
    pieces = [
        window[frame : frame + count, q : q + rows].reshape(count * rows * columns, channels) for q in range(3)
    ]
    return taps(jnp.concatenate(pieces, axis=1), weight, columns).reshape(count, rows, columns, channels)


def edge_taps(edge, weight, q):
    frames, columns, channels = edge.shape[0] - 2, edge.shape[2], edge.shape[3]
    pieces = [edge[t : t + frames, 0].reshape(frames * columns, channels) for t in range(3)]
    return taps(
        jnp.concatenate(pieces, axis=1), lambda r: weight[:, q, r].reshape(3 * channels, channels), columns
    ).reshape(frames, 1, columns, channels)


def earlier_taps(window, weight, result):
    wide = 3 * window.shape[3]
    result[...] += frame_taps(window, lambda r: weight[0, :, r].reshape(wide, -1), 0, 2)
    result[0:1] += frame_taps(window, lambda r: weight[1, :, r].reshape(wide, -1), 1, 1)


def own_kernel(change, own, residual, weight, *refs):
    partial, done, window, source, taken, result, sems = refs[-7:]
    frames, rows, columns, channels = source.shape
    copies = fetch(
        [
            (own, window.at[pl.ds(2, frames), pl.ds(1, rows)]),
            (weight.at[2], taken.at[1]),
            (residual, source),
            (weight.at[1], taken.at[0]),
        ],
        sems,
    )
    empty = jnp.zeros((frames, 1, columns, channels), BF16)
    window[2:, 0:1] = empty
    window[2:, rows + 1 :] = empty
    done[...] = jnp.zeros_like(done)
    copies[0].wait()
    if change:
        for f in range(2, frames + 2):
            window[f, 1 : rows + 1] = act(window[f, 1 : rows + 1].astype(F32)).astype(BF16)
    finish(copies[1:3])
    wide = 3 * channels
    result[...] = source[...].astype(F32) + frame_taps(
        window, lambda r: taken[1, :, r].reshape(wide, channels), 2, 2
    )
    first = fetch([(result.at[0], partial.at[0])], sems.at[pl.ds(4, 1)])
    copies[3].wait()
    result[1] += frame_taps(window, lambda r: taken[0, :, r].reshape(wide, channels), 2, 1)[0]
    finish(first + fetch([(result.at[1], partial.at[1])], sems.at[pl.ds(5, 1)]))


def earlier_kernel(before, own, weight, _, partial, window, result, sems):
    frames, rows, columns, channels = result.shape
    copies = fetch([(before, window.at[:, pl.ds(1, rows)]), (own, result)], sems)
    empty = jnp.zeros((frames, 1, columns, channels), BF16)
    window[:, 0:1] = empty
    window[:, rows + 1 :] = empty
    copies[0].wait()
    for f in range(frames):
        window[f, 1 : rows + 1] = act(window[f, 1 : rows + 1].astype(F32)).astype(BF16)
    copies[1].wait()
    earlier_taps(window, weight, result)
    finish(fetch([(result, partial)], sems.at[pl.ds(2, 1)]))


def both_kernel(before, own, residual, weight, _, partial, window, source, result, sems):
    frames, rows, columns, channels = source.shape
    copies = fetch(
        [
            (own, window.at[pl.ds(2, frames), pl.ds(1, rows)]),
            (residual, source),
            (before, window.at[pl.ds(0, 2), pl.ds(1, rows)]),
        ],
        sems,
    )
    empty = jnp.zeros((frames + 2, 1, columns, channels), BF16)
    window[:, 0:1] = empty
    window[:, rows + 1 :] = empty
    finish(copies)
    wide = 3 * channels
    result[...] = source[...].astype(F32) + frame_taps(
        window, lambda r: weight[2, :, r].reshape(wide, channels), 2, 2
    )
    result[1:2] += frame_taps(window, lambda r: weight[1, :, r].reshape(wide, channels), 2, 1)
    earlier_taps(window, weight, result)
    finish(fetch([(result, partial)], sems.at[pl.ds(3, 1)]))


def rest(change, up, down, partial, weight, edges, total, sems):
    copies = fetch([(up, edges.at[0]), (down, edges.at[1]), (partial, total)], sems)
    finish(copies[:2])
    if change:
        edges[...] = act(edges[...].astype(F32)).astype(BF16)
    copies[2].wait()
    total[:, 0:1] += edge_taps(edges.at[0], weight, 0)
    total[:, -1:] += edge_taps(edges.at[1], weight, 2)


def first_kernel(
    up, down, partial, weight, codes, others, first, active, codes_out, done, edges, total, a, b, sems
):
    done[...] = jnp.zeros_like(done)
    double(codes, others, codes_out)
    rest(True, up, down, partial, weight, edges, total, sems)
    outs = []
    for f in range(total.shape[0]):
        a[f] = total[f].astype(BF16)
        b[f] = act(a[f].astype(F32)).astype(BF16)
        for i, (src, dst) in enumerate(((b, active), (a, first))):
            outs.append(pltpu.make_async_copy(src.at[f], dst.at[f], sems.at[4 + 2 * f + i]))
            outs[-1].start()
    finish(outs)


def second_kernel(up, down, partial, weight, place, codes, others, *refs):
    encoded, terms, codes_out, done, edges, total, a, packed, sems = refs
    done[...] = jnp.zeros_like(done)
    double(codes, others, codes_out)
    rest(False, up, down, partial, weight, edges, total, sems)
    frames, rows, columns, channels = total.shape
    a[...] = total[...].astype(BF16)
    outs = fetch([(a, encoded)], sems.at[pl.ds(4, 1)])
    flat = a[...].reshape(frames * rows * columns, channels)
    cells = flat.shape[0]
    step = BLOCK
    at_slot = rows16(cells)
    slot = place[0:1, :].astype(jnp.int32)
    for i in range(packed.shape[0] // step):
        mine = onehot16(at_slot == (slot - i * step).astype(jnp.int16))
        span = pl.ds(i * step, step)
        packed[span, :] = jnp.dot(mine, flat, preferred_element_type=F32).astype(BF16)
        outs.append(pltpu.make_async_copy(packed.at[span], terms.at[span], sems.at[5 + i]))
        outs[-1].start()
    finish(outs)


def rotate_kernel(place, encoded, upstream, *refs):
    found, (grad, rows_in, e_in, g_in, out, sems) = refs[:-6], refs[-6:]
    size = found[0].shape[0]
    parts = [(part, rows_in.at[pl.ds(k * size, size)]) for k, part in enumerate(found)]
    copies = fetch([(encoded, e_in), (upstream, g_in)] + parts, sems)
    cells, slots = out.shape[0], rows_in.shape[0]
    column = place[...].T[:, 1:2]
    finish(copies)
    step = 256
    for i in range(cells // step):
        span = slice(i * step, (i + 1) * step)
        mine = onehot(lax.broadcasted_iota(jnp.int32, (step, slots), 1).astype(F32) == column[span])
        q = jnp.dot(mine, rows_in[...], preferred_element_type=F32)
        e = e_in[span, :].astype(F32)
        g = g_in[span, :].astype(F32)
        lat_norm = jnp.sqrt(jnp.sum(e * e, -1, keepdims=True) + 1e-06)
        quant_norm = jnp.sqrt(jnp.sum(q * q, -1, keepdims=True) + 1e-06)
        a = e / lat_norm
        b = q / quant_norm
        cosine = jnp.sum(a * b, -1, keepdims=True)
        s = a + b
        turned = g - s * (jnp.sum(s * g, -1, keepdims=True) / (1.0 + cosine))
        turned = turned + 2.0 * a * jnp.sum(b * g, -1, keepdims=True)
        out[span, :] = (quant_norm / lat_norm * turned + 2.0 * COMMIT * (e - q)).astype(BF16)
    finish(fetch([(out, grad)], sems.at[pl.ds(0, 1)]))


def sort_kernel(tiles, capacity, near, here, every, bounds_ref, order_ref, sorted_ref, named_ref, codes_ref):
    groups = every.shape[0] // tiles
    for k in range(tiles):
        codes_ref[pl.ds((near[0] ^ k) * groups, groups)] = every[k * groups : (k + 1) * groups]
    sources, lines, width = codes_ref.shape
    rows = bounds_ref.shape[0] * BLOCK
    mine = (here[0] * tiles + near[0]) * rows
    cells = lines * width
    slots = sources * capacity
    blocks = bounds_ref.shape[0]
    chunks = slots // BLOCK
    earlier = onehot(
        lax.broadcasted_iota(jnp.int32, (width, width), 0) < lax.broadcasted_iota(jnp.int32, (width, width), 1)
    )
    parts, ranks = [], []
    before = jnp.zeros((sources, 1), F32)
    for i in range(lines):
        local = codes_ref[:, i, :] - mine
        inside = (local >= 0) & (local < rows)
        part = jnp.where(inside, 1.0, 0.0)
        rank = jnp.dot(part.astype(BF16), earlier, preferred_element_type=F32) + before
        before = before + jnp.sum(part, 1, keepdims=True)
        parts.append(jnp.where(inside, local, -1))
        ranks.append(jnp.where(inside, rank, -1.0))
    parts, ranks = jnp.concatenate(parts, axis=1), jnp.concatenate(ranks, axis=1)
    picked_high = jnp.where(parts >= 0, parts // 256, 0).astype(F32)
    picked_low = jnp.where(parts >= 0, parts % 256, 0).astype(F32)
    picked_one = jnp.where(parts >= 0, 1.0, 0.0)
    slot = lax.broadcasted_iota(jnp.int32, (capacity, cells), 0).astype(F32)
    found = []
    for i in range(sources):
        span = slice(i, i + 1)
        picked = jnp.concatenate(
            [picked_high[span], picked_low[span], picked_one[span], jnp.zeros((5, cells), F32)], axis=0
        )
        found.append(
            lax.dot_general(picked.astype(BF16), onehot(slot == ranks[span]), NT, preferred_element_type=F32)
        )
    found = jnp.concatenate(found, axis=1)
    code = jnp.where(found[2:3] > 0.5, found[0:1] * 256.0 + found[1:2], -1.0).astype(jnp.int32)
    block = jnp.where(code >= 0, code // BLOCK, -1)
    hits = jnp.where(lax.broadcasted_iota(jnp.int32, (blocks, slots), 0) == block, 1.0, 0.0)
    before = jnp.zeros((blocks, 1), F32)
    parts = []
    for i in range(slots // width):
        part = hits[:, i * width : (i + 1) * width]
        parts.append(jnp.dot(part.astype(BF16), earlier, preferred_element_type=F32) + before)
        before = before + jnp.sum(part, 1, keepdims=True)
    ranks = jnp.concatenate(parts, axis=1)
    counts = lax.dot_general(jnp.ones((8, slots), BF16), hits.astype(BF16), NT, preferred_element_type=F32)[0:1]
    lower = lax.broadcasted_iota(jnp.int32, (blocks, blocks), 1) < lax.broadcasted_iota(jnp.int32, (blocks, blocks), 0)
    starts = jnp.sum(jnp.where(lower, counts, 0.0), 1, keepdims=True)
    lane = lax.broadcasted_iota(jnp.int32, (blocks, width), 1)
    bounds_ref[...] = jnp.where(lane == 0, starts, starts + before).astype(jnp.int32)
    order = jnp.sum(hits * (ranks + starts), 0, keepdims=True)
    order = jnp.where(code >= 0, order, -1.0)
    order_ref[...] = order
    at = order.astype(jnp.int32)
    chunk = lax.broadcasted_iota(jnp.int32, (chunks, slots), 0) == jnp.where(at >= 0, at // BLOCK, -1)
    ones = jnp.where(chunk, 1.0, 0.0)
    picked = jnp.concatenate(
        [ones * (code // BLOCK).astype(F32), ones * (code % BLOCK).astype(F32), ones], axis=0
    ).astype(BF16)
    chosen = onehot(lax.broadcasted_iota(jnp.int32, (BLOCK, slots), 0) == at % BLOCK)
    spread = lax.dot_general(picked, chosen, NT, preferred_element_type=F32)
    inside = jnp.where(
        spread[2 * chunks :] > 0.5, spread[:chunks] * float(BLOCK) + spread[chunks : 2 * chunks], -1.0
    )
    sorted_ref[...] = jnp.full(sorted_ref.shape, -1, jnp.int32)
    sorted_ref[:chunks, :] = inside.astype(jnp.int32)
    low = onehot(lax.broadcasted_iota(jnp.int32, (BLOCK, slots), 0) == jnp.where(code >= 0, code % BLOCK, -1))
    named = lax.dot_general(low, hits.astype(BF16), NT, preferred_element_type=F32)
    named_ref[...] = jnp.zeros(named_ref.shape, F32)
    named_ref[:, :blocks] = named


def scatter_kernel(here, bounds, terms, book, order, codes, named, grad, rows_in, book_in, ranked, out, sums, sems):
    slots = rows_in.shape[0]
    chunks = slots // BLOCK
    blocks = out.shape[0] // BLOCK
    own = pl.ds(pl.multiple_of(here[0] * out.shape[0], BLOCK), out.shape[0])
    copies = fetch([(terms, rows_in), (book.at[own], book_in)], sems)
    ranked[slots:, :] = jnp.zeros((ranked.shape[0] - slots, ranked.shape[1]), BF16)
    at_slot = rows16(slots)
    place = order[...].astype(jnp.int32)
    copies[0].wait()
    for i in range(chunks):
        span = slice(i * BLOCK, (i + 1) * BLOCK)
        mine = onehot16(at_slot == (place - i * BLOCK).astype(jnp.int16))
        ranked[span, :] = jnp.dot(mine, rows_in[...], preferred_element_type=F32).astype(BF16)
    copies[1].wait()
    at_row = rows16(2 * BLOCK)

    def two(b, j):
        code = jnp.concatenate([codes[pl.ds(j, 1), :], codes[pl.ds(j + 1, 1), :]], axis=1)
        mine = onehot16(at_row == (code - b * BLOCK).astype(jnp.int16))
        rows = ranked[pl.ds(pl.multiple_of(j * BLOCK, BLOCK), 2 * BLOCK), :]
        return jnp.dot(mine, rows, preferred_element_type=F32)

    def leave(b):
        span = pl.ds(pl.multiple_of(b * BLOCK, BLOCK), BLOCK)
        return pltpu.make_async_copy(out.at[span], grad.at[span], sems.at[2 + b])

    for b in range(blocks):
        span = slice(b * BLOCK, (b + 1) * BLOCK)
        total = two(b, bounds[b, 0] // BLOCK)
        out[span, :] = (2.0 * (named[:, b : b + 1] * book_in[span, :].astype(F32) - total)).astype(BF16)
        leave(b).start()

    def last(b, carry):
        first = bounds[b, 0] // BLOCK
        after = (bounds[b, 1] + BLOCK - 1) // BLOCK
        leave(b).wait()

        @pl.when(after > first + 2)
        def _():
            span = pl.ds(pl.multiple_of(b * BLOCK, BLOCK), BLOCK)
            sums[...] = jnp.zeros_like(sums)

            def more(i, carry):
                sums[...] += two(b, first + 2 * i)
                return carry

            lax.fori_loop(0, (after - first + 1) // 2, more, 0)
            counts = pltpu.roll(named[...], lax.rem(named.shape[1] - b, named.shape[1]), 1)
            out[span, :] = (2.0 * (counts[:, 0:1] * book_in[span, :].astype(F32) - sums[...])).astype(BF16)
            leave(b).start()
            leave(b).wait()

        return carry

    lax.fori_loop(0, blocks, last, 0)


def shape(dims, dtype=BF16):
    return jax.ShapeDtypeStruct(tuple(dims), dtype)


def halo(video, after, codes, others):
    before = along(video, "tm", 1)
    frames, _, columns, channels = video.shape
    both = shape((2 * frames, 1, columns, channels))
    more = shape((2 * codes.shape[0],) + codes.shape[1:], jnp.int32)
    top, bottom, codes, done = pl.pallas_call(
        join_kernel,
        out_shape=(both, both, more, shape((8, 128), F32)),
        in_specs=[HBM] * 2 + [VMEM] * 3,
        out_specs=(HBM, HBM, VMEM, VMEM),
        scratch_shapes=[pltpu.VMEM((2,) + both.shape, BF16), pltpu.SemaphoreType.DMA((6,))],
        compiler_params=params(),
    )(before, video, after, codes, others)
    return before, along(bottom, "height", 1), along(top, "height", -1), codes, done


def swapped(codes, axis, by):
    count = lax.axis_size(axis)
    return lax.ppermute(codes, axis, [(i, i ^ by) for i in range(count)])


def on_device(latents, conv_first, conv_second, codebook, codes, upstream):
    frames, rows, columns, channels = latents.shape
    cells = frames * rows * columns
    held = codebook.shape[0]
    tiles = lax.axis_size("tm")
    groups = lax.axis_size("height")
    owners = tiles * groups
    range_rows = held // tiles
    capacity = 2 * cells // owners
    slots = owners * capacity
    block = (frames, rows, columns, channels)
    window = pltpu.VMEM((frames + 2, rows + 2, columns, channels), BF16)
    edges = pltpu.VMEM((2, frames + 2, 1, columns, channels), BF16)
    whole = pltpu.VMEM(block, F32)
    half = pltpu.VMEM(block, BF16)
    token = shape((8, 128), F32)
    sems = pltpu.SemaphoreType.DMA
    near = lax.axis_index("tm").astype(jnp.int32).reshape(1)
    here = lax.axis_index("height").astype(jnp.int32).reshape(1)

    def code_lines(count):
        return shape((count * groups, frames * rows, columns), jnp.int32)

    shared = lax.all_gather(codes.reshape(frames * rows, columns), "height")
    ask, low, place = pl.pallas_call(
        functools.partial(index_kernel, groups, tiles, held, capacity),
        out_shape=(
            shape((slots // BATCH, BATCH), jnp.int32),
            shape((BATCH, slots // BATCH), F32),
            shape((8, cells), F32),
        ),
        in_specs=[SMEM, VMEM],
        out_specs=(VMEM,) * 3,
        compiler_params=params(),
    )(here, shared)
    every = shared
    by = 1
    while by * 8 < tiles:
        every = jnp.concatenate([every, swapped(every, "tm", by)])
        by *= 2
    partial, done = pl.pallas_call(
        functools.partial(own_kernel, True),
        out_shape=(shape(block, F32), token),
        in_specs=[HBM] * 4,
        out_specs=(HBM, VMEM),
        scratch_shapes=[window, half, pltpu.VMEM((2, 3, 3, channels, channels), BF16), whole, sems((6,))],
        compiler_params=params(28),
    )(latents, latents, conv_first, place)
    before, up, down, _, done = halo(latents, done, shared, shared)
    partial = pl.pallas_call(
        earlier_kernel,
        out_shape=shape(block, F32),
        in_specs=[HBM] * 2 + [VMEM] * 2,
        out_specs=HBM,
        scratch_shapes=[pltpu.VMEM((2, rows + 2, columns, channels), BF16), whole, sems((3,))],
        compiler_params=params(),
    )(before, partial, conv_first, done)
    first, active, every, done = pl.pallas_call(
        first_kernel,
        out_shape=(shape(block), shape(block), code_lines(2 * by), token),
        in_specs=[HBM] * 3 + [VMEM] * 3,
        out_specs=(HBM, HBM, VMEM, VMEM),
        scratch_shapes=[edges, whole, half, half, sems((4 + 2 * frames,))],
        compiler_params=params(),
    )(up, down, partial, conv_first, every, swapped(every, "tm", by))
    by *= 2

    def lookup(which, after):
        return pl.pallas_call(
            functools.partial(gather_kernel, which),
            out_shape=(shape((slots // groups, channels)),) * len(which) + (token,),
            in_specs=[SMEM, HBM, VMEM, VMEM],
            out_specs=(HBM,) * len(which) + (VMEM,),
            scratch_shapes=[
                pltpu.VMEM((slots // groups * len(which), TILE, channels), BF16),
                pltpu.VMEM((slots // groups * len(which), channels), BF16),
                sems((slots // groups * len(which) // BATCH,)),
                sems((len(which),)),
            ],
            compiler_params=params(),
        )(ask, codebook.reshape(held // TILE, TILE, channels), low, after)

    *found, done = lookup(range(1, groups), done)
    before, up, down, every, done = halo(active, done, every, swapped(every, "tm", by))
    by *= 2
    partial = pl.pallas_call(
        both_kernel,
        out_shape=shape(block, F32),
        in_specs=[HBM] * 3 + [VMEM] * 2,
        out_specs=HBM,
        scratch_shapes=[window, half, whole, sems((4,))],
        compiler_params=params(),
    )(before, active, first, conv_second, done)
    encoded, terms, every, done = pl.pallas_call(
        second_kernel,
        out_shape=(shape(block), shape((slots, channels)), code_lines(2 * by), token),
        in_specs=[HBM] * 3 + [VMEM] * 4,
        out_specs=(HBM, HBM, VMEM, VMEM),
        scratch_shapes=[edges, whole, half, pltpu.VMEM((slots, channels), BF16), sems((5 + slots // 256,))],
        compiler_params=params(),
    )(up, down, partial, conv_second, place, every, swapped(every, "tm", by))

    owner_terms = lax.all_to_all(
        terms.reshape(owners, capacity, channels), ("tm", "height"), split_axis=0, concat_axis=0, tiled=True
    )
    found = [around(rows_of, "height", k + 1) for k, rows_of in enumerate(found)]
    found = [lookup(range(1), done)[0]] + found
    blocks = range_rows // BLOCK
    chunks = slots // BLOCK
    bounds, order, ranked, named = pl.pallas_call(
        functools.partial(sort_kernel, tiles, capacity),
        out_shape=(
            shape((blocks, 128), jnp.int32),
            shape((1, slots), F32),
            shape((-(-(chunks + 2) // 8) * 8, BLOCK), jnp.int32),
            shape((BLOCK, 128), F32),
        ),
        in_specs=[SMEM, SMEM, VMEM],
        out_specs=(VMEM,) * 4,
        scratch_shapes=[pltpu.VMEM((owners, frames * rows, columns), jnp.int32)],
        compiler_params=params(),
    )(near, here, every)
    grad = pl.pallas_call(
        rotate_kernel,
        out_shape=shape((cells, channels)),
        in_specs=[VMEM] + [HBM] * (2 + groups),
        out_specs=HBM,
        scratch_shapes=[pltpu.VMEM((slots, channels), BF16)] + [pltpu.VMEM((cells, channels), BF16)] * 3
        + [sems((2 + groups,))],
        compiler_params=params(),
    )(
        place,
        encoded.reshape(cells, channels),
        upstream.reshape(cells, channels),
        *found,
    )
    codebook_grad = pl.pallas_call(
        scatter_kernel,
        out_shape=shape((range_rows, channels)),
        in_specs=[SMEM, SMEM, HBM, HBM, VMEM, VMEM, VMEM],
        out_specs=HBM,
        scratch_shapes=[
            pltpu.VMEM((slots, channels), BF16),
            pltpu.VMEM((range_rows, channels), BF16),
            pltpu.VMEM((slots + 2 * BLOCK, channels), BF16),
            pltpu.VMEM((range_rows, channels), BF16),
            pltpu.VMEM((BLOCK, channels), F32),
            sems((2 + blocks,)),
        ],
        compiler_params=params(),
    )(near, bounds, owner_terms.reshape(slots, channels), codebook, order, ranked, named)
    return (grad.reshape(upstream.shape), codebook_grad)


def solution(mesh):
    return jax.shard_map(
        on_device,
        mesh=mesh,
        in_specs=(
            P("tm", "height", None, None),
            P(),
            P(),
            P("height", None),
            P("tm", "height", None),
            P("tm", "height", None, None),
        ),
        out_specs=(P("tm", "height", None, None), P(("height", "tm"), None)),
        check_vma=False,
    )
```
